32 devices in a mesh: brick: 16 (over z, y, x), state: 2 (over core).
Axes of the slice: x: 2, y: 2, z: 4, core: 2. Of those that a mesh axis runs over, the one named last changes fastest.
Arguments:
- states: bfloat16 [384, 110592], P('state', 'brick'), may hold values from -40 to 40
- kinetic: bfloat16 [343, 343], replicated, may hold values from -2 to 4, as said below
- potential: float32 [110592], P('brick'), may hold values from -1.5 to 1.5
- cell_nodes: int32 [512, 343], P('brick'), may hold values from 0 to 8063, as said below
- face_map: int32 [18432], P('brick'), may hold values from 0 to 6911, as said below
Outputs:
- rotated: float32 [384, 110592], P('state', 'brick')
The draws below stay inside these ranges and needn't reach their ends.
Inputs may be any that keep to these rules, and one draw needn't show every extreme that they name: `cell_nodes`: block b of 32 rows belongs to brick b; a row lists the 343 nodes of one hexahedral cell of degree 6, lexicographic in the cell's three local coordinates, the first slowest. A value below 6912 is a column of brick b's block of states and potential; a value 6912 + f is the node named by entry f of brick b + 1's block of face_map (brick 0 after the last). Every own node and every face slot lies in some cell. `face_map`: block b of 1152 entries lists distinct own nodes of brick b: those it shares with brick b - 1. `kinetic`: Symmetric.
All inputs are finite; a program needn't handle non-finite values.
Results may differ from the reference program's by a relative error of at most 0.0005.
The reference program's roundings to bfloat16 on the way (of `filtered_once`, `filtered` and `root_rounded`) count: a program that leaves them out, or rounds other values in their place, can miss the bound.
Values may be sent and summed in bfloat16 or wider, within the bound.
No kernel may reach another device: no remote copies, remote signals or barrier semaphores. Data moves between devices by JAX's collectives and lax.ppermute only.
A program may use at most 128 MiB of HBM per device.

```python
import math
import jax
import jax.numpy as jnp
from jax import lax

DEG = 6
STATES = 384
CX = 1
CY = 4
CZ = 8
NS_STEPS = 3
CELLS = 32
OWN = 6912
FACE = 1152
NODES = 110592
CELLS_ALL = 512
FACES_ALL = 18432
N_BRICK = 16


def brick_numbering(key, brick_id):
    brick_seed = jax.random.fold_in(jax.random.fold_in(key, 7311), brick_id)
    numbering = jax.random.permutation(brick_seed, OWN).astype(jnp.int32)
    top_at = jnp.argmax(numbering == OWN - 1)
    numbering = numbering.at[top_at].set(numbering[0]).at[0].set(OWN - 1)
    low_at = jnp.argmax(numbering == 0)
    numbering = numbering.at[low_at].set(numbering[1]).at[1].set(0)
    return numbering


def brick_cells(key, brick_id):
    numbering = brick_numbering(key, brick_id)
    side_x = DEG * CX
    side_y = DEG * CY
    side_z = DEG * CZ
    cell_seed = jax.random.fold_in(jax.random.fold_in(key, 9157), brick_id)
    cell_order = jax.random.permutation(cell_seed, CELLS).astype(jnp.int32)
    cell_x = cell_order // (CY * CZ)
    cell_y = cell_order // CZ % CY
    cell_z = cell_order % CZ
    local_node = jnp.arange((DEG + 1) ** 3, dtype=jnp.int32)
    along_x = local_node // (DEG + 1) ** 2
    along_y = local_node // (DEG + 1) % (DEG + 1)
    along_z = local_node % (DEG + 1)
    plane_x = DEG * cell_x[:, None] + along_x[None, :]
    row_y = (DEG * cell_y[:, None] + along_y[None, :]) % side_y
    row_z = (DEG * cell_z[:, None] + along_z[None, :]) % side_z
    canonical = (jnp.minimum(plane_x, side_x - 1) * side_y + row_y) * side_z + row_z
    return jnp.where(plane_x < side_x, numbering[canonical], OWN + row_y * side_z + row_z).astype(jnp.int32)


def draw_cell_nodes(key, part):
    bricks = CELLS_ALL // CELLS
    blocks = jax.vmap(lambda brick_id: brick_cells(key, brick_id))(jnp.arange(bricks, dtype=jnp.int32))
    return blocks.reshape(CELLS_ALL, (DEG + 1) ** 3)


def draw_face_map(key, part):
    bricks = CELLS_ALL // CELLS
    blocks = jax.vmap(lambda brick_id: brick_numbering(key, brick_id)[:FACE])(jnp.arange(bricks, dtype=jnp.int32))
    return blocks.reshape(FACES_ALL)


def draw_states(key, part):
    bricks = CELLS_ALL // CELLS
    base_key = jax.random.fold_in(key, 0)
    column_key = jax.random.fold_in(key, 1)
    mixing_key = jax.random.fold_in(key, 4)
    brick_of_node = (jnp.arange(NODES) // OWN).astype(jnp.float32)
    node_scale = 1.0 + 2.0 * brick_of_node / max(bricks - 1, 1)
    state_scale = jnp.exp(jax.random.uniform(column_key, (STATES,), minval=math.log(0.3), maxval=math.log(3.0)))
    values = jnp.clip(jax.random.normal(base_key, (STATES, NODES)), -4.0, 4.0)
    blocks = values.reshape(STATES, bricks, OWN).transpose(1, 0, 2)

    def mix_one(inputs):
        brick_id, block = inputs
        noise = jnp.clip(jax.random.normal(jax.random.fold_in(mixing_key, brick_id), (STATES, STATES)), -4.0, 4.0)
        mixing = jnp.eye(STATES, dtype=jnp.float32) + 0.7 * noise / math.sqrt(STATES)
        return jnp.dot(mixing, block, precision=lax.Precision.HIGHEST)
    mixed_blocks = lax.map(mix_one, (jnp.arange(bricks, dtype=jnp.int32), blocks))
    mixed = mixed_blocks.transpose(1, 0, 2).reshape(STATES, NODES)
    result = mixed * state_scale[:, None] * node_scale[None, :]
    return jnp.clip(result, -40.0, 40.0).astype(jnp.bfloat16)


def draw_kinetic(key, part):
    width = (DEG + 1) ** 3
    first_key, second_key = jax.random.split(key, 2)
    noise = jnp.clip(jax.random.normal(first_key, (width, width)), -4.0, 4.0)
    symmetric = 0.5 * (noise + noise.T) / math.sqrt(width)
    diagonal = jnp.exp(jax.random.uniform(second_key, (width,), minval=math.log(0.3), maxval=math.log(1.5)))
    return (symmetric + jnp.diag(diagonal)).astype(jnp.bfloat16)


def block_levels(stream_key, shape, cuts, least, largest):
    gain = 1.0
    for dim, shards_of in cuts:
        heights = jax.random.uniform(jax.random.fold_in(jax.random.fold_in(stream_key, 6), dim), (shards_of,), jnp.float32, least / len(cuts), largest / len(cuts))
        gain = gain * jnp.repeat(jnp.exp(heights), shape[dim] // shards_of).reshape((-1,) + (1,) * (len(shape) - 1 - dim))
    return gain


def setup_inputs(seed: int = 0) -> dict:
    arg_keys = jax.random.split(jax.random.key(seed), 6)
    return {
        "states": draw_states(jax.random.fold_in(arg_keys[5], 71), 0),
        "kinetic": draw_kinetic(jax.random.fold_in(arg_keys[5], 71), 0),
        "potential": jnp.clip(jax.random.uniform(arg_keys[2], (NODES,), jnp.float32, -1.5, 1.5) * block_levels(arg_keys[2], (NODES,), ((0, 16),), -0.4, 0.0), -1.5, 1.5),
        "cell_nodes": draw_cell_nodes(jax.random.fold_in(arg_keys[5], 71), 0),
        "face_map": draw_face_map(jax.random.fold_in(arg_keys[5], 71), 0),
    }


cheb_center = 3.0
cheb_half = 7.0
epsilon = 1e-06

def global_numbering(cell_nodes, face_map):
    brick_of_cell = (jnp.arange(CELLS_ALL, dtype=jnp.int32) // CELLS)[:, None]
    next_brick = (brick_of_cell + 1) % N_BRICK
    is_ghost = cell_nodes >= OWN
    face_slot = jnp.clip(cell_nodes - OWN, 0, FACE - 1).astype(jnp.int32)
    ghost_target = face_map[(next_brick * FACE + face_slot).astype(jnp.int32)]
    return jnp.where(is_ghost, next_brick * OWN + ghost_target, brick_of_cell * OWN + cell_nodes).astype(jnp.int32)

def apply_operator(vector, kinetic, potential, global_nodes):
    total_nodes, width = vector.shape
    block_width = math.gcd(width, 64)
    kinetic_wide = kinetic.astype(jnp.float32)
    index_table = global_nodes.T
    flat_index = index_table.reshape(-1)
    per_cell = kinetic.shape[0]

    def one_block(column_block):
        gathered = column_block[index_table].astype(jnp.float32).reshape(per_cell, -1)
        products = jnp.dot(kinetic_wide, gathered, precision=lax.Precision.HIGHEST, preferred_element_type=jnp.float32)
        return jax.ops.segment_sum(products.reshape(-1, block_width), flat_index, num_segments=total_nodes)
    pieces = vector.reshape(total_nodes, width // block_width, block_width).transpose(1, 0, 2)
    result = lax.map(one_block, pieces).transpose(1, 0, 2).reshape(total_nodes, width)
    return result + potential[:, None] * vector.astype(jnp.float32)

def newton_schulz(margin):
    total = margin.shape[0]
    identity = jnp.eye(total, dtype=margin.dtype)
    scale = jnp.sqrt(jnp.sum(margin * margin) + epsilon)
    current = margin / scale
    inverse = identity
    for iteration in range(NS_STEPS):
        factor = 3.0 * identity - jnp.dot(inverse, current, precision=lax.Precision.HIGHEST)
        current = 0.5 * jnp.dot(factor, current, precision=lax.Precision.HIGHEST)
        inverse = 0.5 * jnp.dot(factor, inverse, precision=lax.Precision.HIGHEST)
    return inverse

def reference(states, kinetic, potential, cell_nodes, face_map):
    node_major = states.T
    global_nodes = global_numbering(cell_nodes, face_map)
    first = apply_operator(node_major, kinetic, potential, global_nodes)
    filtered_once = ((first - cheb_center * node_major.astype(jnp.float32)) / cheb_half).astype(jnp.bfloat16)
    second = apply_operator(filtered_once, kinetic, potential, global_nodes)
    filtered = (2.0 * (second - cheb_center * filtered_once.astype(jnp.float32)) / cheb_half - node_major.astype(jnp.float32)).astype(jnp.bfloat16)
    wide = filtered.astype(jnp.float32)
    margin = lax.dot_general(wide, wide, (((0,), (0,)), ((), ())), precision=lax.Precision.HIGHEST, preferred_element_type=jnp.float32)
    inverse_root = newton_schulz(margin)
    root_rounded = inverse_root.astype(jnp.bfloat16).astype(jnp.float32)
    return lax.dot_general(root_rounded, wide, (((1,), (1,)), ((), ())), precision=lax.Precision.HIGHEST, preferred_element_type=jnp.float32)
```

```python
import functools
import jax
import jax.numpy as jnp
from jax import lax
from jax.experimental import pallas as pl
from jax.experimental.pallas import tpu as pltpu
from jax.sharding import PartitionSpec as P

NS_STEPS = 3
LANES = 128
BATCH = 16

cheb_center = 3.0
cheb_half = 7.0
epsilon = 1e-06

VMEM = pl.BlockSpec(memory_space=pltpu.VMEM)
SMEM = pl.BlockSpec(memory_space=pltpu.SMEM)
ANY = pl.BlockSpec(memory_space=pl.ANY)


def params(limit=40):
    return pltpu.CompilerParams(vmem_limit_bytes=limit << 20)


def passed_along(value, axis, steps):
    count = lax.axis_size(axis)
    pairs = [(source, (source + steps) % count) for source in range(count)]
    return lax.ppermute(value, axis, pairs)


def block_of(count):
    for size in (256, 128):
        if count % size == 0:
            return size
    return count


def identity(size):
    rows = lax.broadcasted_iota(jnp.int32, (size, size), 0)
    columns = lax.broadcasted_iota(jnp.int32, (size, size), 1)
    return (rows == columns).astype(jnp.bfloat16)


def across(left, right):
    return lax.dot_general(left, right, (((1,), (1,)), ((), ())), preferred_element_type=jnp.float32)


def split3(wide):
    first = wide.astype(jnp.bfloat16)
    rest = wide - first.astype(jnp.float32)
    second = rest.astype(jnp.bfloat16)
    third = (rest - second.astype(jnp.float32)).astype(jnp.bfloat16)
    return first, second, third


def across_wide(unit, wide):
    first, second, third = split3(wide)
    return across(unit, first) + (across(unit, second) + across(unit, third))


def padded_rows(block):
    width = block.shape[0]
    return jnp.concatenate([block, jnp.zeros((2 * LANES - width, block.shape[1]), block.dtype)], axis=0)


def store_nodes(ref, start, block, values):
    ref[pl.ds(2 * start, block, 2), :] = values[:, :LANES]
    ref[pl.ds(2 * start + 1, block, 2), :] = values[:, LANES:]


def load_nodes(ref, start, block):
    return jnp.concatenate([ref[pl.ds(2 * start, block, 2), :], ref[pl.ds(2 * start + 1, block, 2), :]], axis=1)


def pack(ref, count, width):
    low = ref[pl.ds(0, count, 2), :]
    high = ref[pl.ds(1, count, 2), :]
    rest = width - LANES
    fold = LANES // rest
    part = count // fold
    return low, jnp.concatenate([high[i * part : (i + 1) * part, :rest] for i in range(fold)], axis=1)


def unpack(packed, count, width):
    rest = width - LANES
    fold = LANES // rest
    part = count // fold
    low = packed[:count]
    high = jnp.concatenate([packed[count:, i * rest : (i + 1) * rest] for i in range(fold)], axis=0)
    return low, jnp.concatenate([high, jnp.zeros((count, LANES - rest), high.dtype)], axis=1)


def gather_face(face, source, target, count):
    step = 64

    def some(i, _):
        base = i * step
        for j in range(step):
            target[pl.ds(pl.multiple_of(2 * (base + j), 2), 2), :] = source[
                pl.ds(pl.multiple_of(face[base + j], 2), 2), :
            ]
        return 0

    lax.fori_loop(0, count // step, some, 0)


def add_face(face, source, target, count):
    step = BATCH

    def some(i, _):
        base = i * step
        places = [pl.multiple_of(face[base + j], 2) for j in range(step)]
        rows = [target[pl.ds(place, 2), :] for place in places]
        for j in range(step):
            target[pl.ds(places[j], 2), :] = rows[j] + source[pl.ds(pl.multiple_of(2 * (base + j), 2), 2), :]
        return 0

    lax.fori_loop(0, count // step, some, 0)


def prepare_kernel(width, face, states, potential, nodes, start, send, picked):
    owned = states.shape[1]
    count = face.shape[0]
    block = block_of(owned)
    unit = identity(block)

    def one(i, _):
        first = pl.multiple_of(i * block, block)
        mine = states[:, pl.ds(first, block)]
        store_nodes(nodes, first, block, across(unit, padded_rows(mine)))
        local = mine.astype(jnp.float32) * (potential[:, pl.ds(first, block)] - cheb_center)
        store_nodes(start, first, block, across_wide(unit, padded_rows(local)))
        return 0

    lax.fori_loop(0, owned // block, one, 0)
    gather_face(face, nodes, picked, count)
    low, high = pack(picked, count, width)
    send[:count, :] = low.astype(jnp.bfloat16)
    send[count:, :] = high.astype(jnp.bfloat16)


def operator_kernel(width, slots, cells, with_start, table, kinetic, ghost, nodes_in, *rest):
    if with_start:
        start_in, out, send, nodes, total, gathered, products, sems = rest
    else:
        out, send, nodes, total, gathered, products, sems = rest
    owned2 = nodes_in.shape[0]
    all2 = nodes.shape[0]
    count = (all2 - owned2) // 2
    copies = [pltpu.make_async_copy(nodes_in, nodes.at[pl.ds(0, owned2)], sems.at[0])]
    if with_start:
        copies.append(pltpu.make_async_copy(start_in, total.at[pl.ds(0, owned2)], sems.at[1]))
    for copy in copies:
        copy.start()
    low, high = unpack(ghost[...].astype(jnp.float32), count, width)
    nodes[pl.ds(owned2, count, 2), :] = low
    nodes[pl.ds(owned2 + 1, count, 2), :] = high
    total[pl.ds(owned2, 2 * count), :] = jnp.zeros((2 * count, LANES), jnp.float32)
    if not with_start:
        total[pl.ds(0, owned2), :] = jnp.zeros((owned2, LANES), jnp.float32)
    rows = gathered.shape[0] // 2
    gathered[pl.ds(2 * slots, 2 * (rows - slots)), :] = jnp.zeros((2 * (rows - slots), LANES), jnp.float32)
    for copy in copies:
        copy.wait()
    stride = table.shape[0] // cells

    def one(cell, _):
        mine = table.at[pl.ds(cell * stride, stride)]
        for a in range(slots):
            gathered[pl.ds(2 * a, 2), :] = nodes[pl.ds(pl.multiple_of(mine[a], 2), 2), :]
        values = jnp.concatenate(
            [gathered[pl.ds(0, rows, 2), :], gathered[pl.ds(1, rows, 2), :]], axis=1
        ).astype(jnp.bfloat16)
        result = jnp.dot(kinetic[...], values, preferred_element_type=jnp.float32)
        products[pl.ds(0, rows, 2), :] = result[:, :LANES]
        products[pl.ds(1, rows, 2), :] = result[:, LANES:]
        for begin in range(0, slots, BATCH):
            size = min(BATCH, slots - begin)
            places = [pl.multiple_of(mine[begin + j], 2) for j in range(size)]
            held = [total[pl.ds(place, 2), :] for place in places]
            for j in range(size):
                total[pl.ds(places[j], 2), :] = held[j] + products[pl.ds(2 * (begin + j), 2), :]
        return 0

    lax.fori_loop(0, cells, one, 0)
    back = pltpu.make_async_copy(total.at[pl.ds(0, owned2)], out, sems.at[0])
    back.start()
    low, high = pack(total.at[pl.ds(owned2, 2 * count)], count, width)
    send[:count, :] = low
    send[count:, :] = high
    back.wait()


def once_kernel(width, face, total, returned, nodes, send, spread, picked, sem):
    count = face.shape[0]
    copy = pltpu.make_async_copy(total, nodes, sem)
    copy.start()
    low, high = unpack(returned[...], count, width)
    spread[pl.ds(0, count, 2), :] = low
    spread[pl.ds(1, count, 2), :] = high
    copy.wait()
    add_face(face, spread, nodes, count)
    block = 2 * block_of(nodes.shape[0] // 2)

    def one(i, _):
        at = pl.ds(pl.multiple_of(i * block, block), block)
        nodes[at, :] = (nodes[at, :] / cheb_half).astype(jnp.bfloat16).astype(jnp.float32)
        return 0

    lax.fori_loop(0, nodes.shape[0] // block, one, 0)
    gather_face(face, nodes, picked, count)
    low, high = pack(picked, count, width)
    send[:count, :] = low.astype(jnp.bfloat16)
    send[count:, :] = high.astype(jnp.bfloat16)


def twice_kernel(width, face, total_in, returned, nodes, states, potential, filtered, total, spread, sem):
    owned = states.shape[1]
    count = face.shape[0]
    copy = pltpu.make_async_copy(total_in, total, sem)
    copy.start()
    low, high = unpack(returned[...], count, width)
    spread[pl.ds(0, count, 2), :] = low
    spread[pl.ds(1, count, 2), :] = high
    copy.wait()
    add_face(face, spread, total, count)
    block = block_of(owned)
    unit = identity(2 * LANES)

    def one(i, _):
        first = pl.multiple_of(i * block, block)
        at = pl.ds(first, block)
        once = across(unit, load_nodes(nodes, first, block).astype(jnp.bfloat16))[:width]
        summed = across_wide(unit, load_nodes(total, first, block))[:width]
        second = summed + (potential[:, at] - cheb_center) * once
        filtered[:, at] = ((2.0 / cheb_half) * second - states[:, at].astype(jnp.float32)).astype(jnp.bfloat16)
        return 0

    lax.fori_loop(0, owned // block, one, 0)


def summed_over(value, axis):
    count = lax.axis_size(axis)
    place = lax.axis_index(axis)
    radices = []
    left = count
    while left > 1:
        radix = 4 if left % 4 == 0 else 2 if left % 2 == 0 else left
        radices.append(radix)
        left //= radix
    shape = value.shape
    flat = value.reshape(-1, LANES)

    def exchange(stride, radix, give):
        digit = place // stride % radix

        def partner(index, step):
            here = index // stride % radix
            return index + ((here + step) % radix - here) * stride

        got = [
            lax.ppermute(give((digit + step) % radix), axis, [(i, partner(i, step)) for i in range(count)])
            for step in range(1, radix)
        ]
        return digit, got

    stride = 1
    trail = []
    for level, radix in enumerate(radices):
        if level == len(radices) - 1:
            _, got = exchange(stride, radix, lambda to: flat)
            flat = flat + functools.reduce(jnp.add, got)
        else:
            pieces = flat.reshape(radix, -1, LANES)
            take = lambda to: lax.dynamic_index_in_dim(pieces, to, 0, keepdims=False)
            digit, got = exchange(stride, radix, take)
            flat = take(digit) + functools.reduce(jnp.add, got)
            trail.append((stride, radix))
        stride *= radix
    for stride, radix in reversed(trail):
        digit, got = exchange(stride, radix, lambda to: flat)
        stacked = jnp.zeros((radix,) + flat.shape, flat.dtype)
        stacked = lax.dynamic_update_index_in_dim(stacked, flat, digit, 0)
        for step in range(1, radix):
            stacked = lax.dynamic_update_index_in_dim(stacked, got[step - 1], (digit - step) % radix, 0)
        flat = stacked.reshape(-1, LANES)
    return flat.reshape(shape)


def newton_schulz(margin, start, width):
    total = margin.shape[0]
    unit = jnp.eye(total, dtype=jnp.float32)
    scale = jnp.sqrt(jnp.sum(margin * margin) + epsilon)
    current = margin / scale
    product = functools.partial(jnp.dot, precision=lax.Precision.HIGHEST)
    factor = 3.0 * unit - current
    current = 0.5 * product(factor, current)
    inverse = 0.5 * factor
    for iteration in range(1, NS_STEPS - 1):
        factor = 3.0 * unit - product(inverse, current)
        current = 0.5 * product(factor, current)
        inverse = 0.5 * product(factor, inverse)
    rows = lax.dynamic_slice_in_dim(inverse, start, width, 0)
    factor = 3.0 * lax.dynamic_slice_in_dim(unit, start, width, 0) - product(rows, current)
    return 0.5 * product(factor, inverse)


def local(states, kinetic, potential, cell_nodes, face_map):
    width, owned = states.shape
    cells, slots = cell_nodes.shape
    count = face_map.shape[0]
    rows = -(-slots // 8) * 8
    stride = -(-slots // LANES) * LANES
    fold = LANES // (width - LANES)
    packed = count + count // fold
    face = 2 * face_map
    table = jnp.pad(2 * cell_nodes, ((0, 0), (0, stride - slots))).reshape(-1)
    matrix = jnp.pad(kinetic, ((0, rows - slots), (0, rows - slots)))
    lumped = potential[None, :]
    wide = jax.ShapeDtypeStruct((2 * owned, LANES), jnp.float32)
    sent = jax.ShapeDtypeStruct((packed, LANES), jnp.bfloat16)
    sent_wide = jax.ShapeDtypeStruct((packed, LANES), jnp.float32)
    spread = pltpu.VMEM((2 * count, LANES), jnp.float32)

    nodes, begun, send = pl.pallas_call(
        functools.partial(prepare_kernel, width),
        out_shape=(wide, wide, sent),
        in_specs=[SMEM, VMEM, VMEM],
        out_specs=(VMEM, VMEM, VMEM),
        scratch_shapes=[spread],
        compiler_params=params(),
    )(face, states, lumped)

    def operator(nodes, ghost, begun):
        args = (table, matrix, ghost, nodes) + (() if begun is None else (begun,))
        return pl.pallas_call(
            functools.partial(operator_kernel, width, slots, cells, begun is not None),
            out_shape=(wide, sent_wide),
            in_specs=[SMEM, VMEM, VMEM, ANY] + ([] if begun is None else [ANY]),
            out_specs=(ANY, VMEM),
            scratch_shapes=[
                pltpu.VMEM((2 * (owned + count), LANES), jnp.float32),
                pltpu.VMEM((2 * (owned + count), LANES), jnp.float32),
                pltpu.VMEM((2 * rows, LANES), jnp.float32),
                pltpu.VMEM((2 * rows, LANES), jnp.float32),
                pltpu.SemaphoreType.DMA((2,)),
            ],
            compiler_params=params(),
        )(*args)

    total, back = operator(nodes, passed_along(send, "brick", -1), begun)
    nodes, send = pl.pallas_call(
        functools.partial(once_kernel, width),
        out_shape=(wide, sent),
        in_specs=[SMEM, ANY, VMEM],
        out_specs=(VMEM, VMEM),
        scratch_shapes=[spread, spread, pltpu.SemaphoreType.DMA],
        compiler_params=params(),
    )(face, total, passed_along(back, "brick", 1))
    total, back = operator(nodes, passed_along(send, "brick", -1), None)
    filtered = pl.pallas_call(
        functools.partial(twice_kernel, width),
        out_shape=jax.ShapeDtypeStruct((width, owned), jnp.bfloat16),
        in_specs=[SMEM, ANY, VMEM, VMEM, VMEM, VMEM],
        out_specs=VMEM,
        scratch_shapes=[pltpu.VMEM((2 * owned, LANES), jnp.float32), spread, pltpu.SemaphoreType.DMA],
        compiler_params=params(),
    )(face, total, passed_along(back, "brick", 1), nodes, states, lumped)

    halves = lax.axis_size("state")
    place = lax.axis_index("state")
    parts = [filtered] + [passed_along(filtered, "state", step) for step in range(1, halves)]
    blocks = [across(filtered, part) for part in parts]
    reduced = summed_over(jnp.stack(blocks), "brick")
    return finish(reduced, parts, halves, place, width)


def finish(reduced, parts, halves, place, width):
    own_rows = jnp.zeros((halves, width, width), jnp.float32)
    for step in range(halves):
        own_rows = lax.dynamic_update_index_in_dim(own_rows, reduced[step], (place - step) % halves, 0)
    row_block = own_rows.transpose(1, 0, 2).reshape(width, -1)
    margin = jnp.zeros((halves, width, halves * width), jnp.float32)
    margin = lax.dynamic_update_index_in_dim(margin, row_block, place, 0)
    for step in range(1, halves):
        margin = lax.dynamic_update_index_in_dim(
            margin, passed_along(row_block, "state", step), (place - step) % halves, 0
        )
    margin = margin.reshape(halves * width, -1)
    root = newton_schulz(margin, place * width, width).astype(jnp.bfloat16)
    result = 0.0
    for step, part in enumerate(parts):
        columns = lax.dynamic_slice_in_dim(root, (place - step) % halves * width, width, 1)
        result = result + jnp.dot(columns, part, preferred_element_type=jnp.float32)
    return result


def solution(mesh):
    in_specs = (P("state", "brick"), P(), P("brick"), P("brick", None), P("brick"))
    out_specs = P("state", "brick")
    return jax.shard_map(local, mesh=mesh, in_specs=in_specs, out_specs=out_specs, check_vma=False)
```

```python
import functools
import jax
import jax.numpy as jnp
from jax import lax
from jax.experimental import pallas as pl
from jax.experimental.pallas import tpu as pltpu
from jax.sharding import PartitionSpec as P

NS_STEPS = 3
LANES = 128
BATCH = 8

cheb_center = 3.0
cheb_half = 7.0
epsilon = 1e-06

VMEM = pl.BlockSpec(memory_space=pltpu.VMEM)
SMEM = pl.BlockSpec(memory_space=pltpu.SMEM)
ANY = pl.BlockSpec(memory_space=pl.ANY)


def called(kernel, shapes, in_specs, scratch, microseconds, limit, out_specs=None, **options):
    return pl.pallas_call(
        kernel,
        out_shape=shapes,
        in_specs=in_specs,
        out_specs=out_specs or (VMEM,) * len(shapes),
        scratch_shapes=scratch,
        compiler_params=pltpu.CompilerParams(vmem_limit_bytes=limit << 20),
        cost_estimate=pl.CostEstimate(
            flops=int(microseconds * 4e8), bytes_accessed=int(microseconds * 3e6), transcendentals=0
        ),
        **options,
    )


def passed_along(value, axis, steps):
    count = lax.axis_size(axis)
    pairs = [(source, (source + steps) % count) for source in range(count)]
    return lax.ppermute(value, axis, pairs)


def rounded_up(count, unit):
    return -(-count // unit) * unit


def block_of(count):
    for size in (256, 128):
        if count % size == 0:
            return size
    return count


def identity(size):
    rows = lax.broadcasted_iota(jnp.int32, (size, size), 0)
    columns = lax.broadcasted_iota(jnp.int32, (size, size), 1)
    return (rows == columns).astype(jnp.bfloat16)


def across(left, right):
    return lax.dot_general(left, right, (((1,), (1,)), ((), ())), preferred_element_type=jnp.float32)


def across_wide(unit, wide):
    first = wide.astype(jnp.bfloat16)
    rest = wide - first.astype(jnp.float32)
    second = rest.astype(jnp.bfloat16)
    third = (rest - second.astype(jnp.float32)).astype(jnp.bfloat16)
    return across(unit, first) + (across(unit, second) + across(unit, third))


def padded_rows(block):
    width = block.shape[0]
    return jnp.concatenate([block, jnp.zeros((2 * LANES - width, block.shape[1]), block.dtype)], axis=0)


def node_rows(start, count):
    return pl.ds(2 * start, count, 2), pl.ds(2 * start + 1, count, 2)


def pair(row):
    return pl.ds(pl.multiple_of(row, 2), 2)


def pack(low, high, width):
    count = low.shape[0]
    rest = width - LANES
    fold = LANES // rest
    part = count // fold
    return low, jnp.concatenate([high[i * part : (i + 1) * part, :rest] for i in range(fold)], axis=1)


def unpack(packed, count, width):
    rest = width - LANES
    fold = LANES // rest
    low = packed[:count]
    high = jnp.concatenate([packed[count:, i * rest : (i + 1) * rest] for i in range(fold)], axis=0)
    return low, jnp.concatenate([high, jnp.zeros((count, LANES - rest), high.dtype)], axis=1)


def some_rows(count, step, body):
    def one(i, _):
        body(i * step, step)
        return 0

    lax.fori_loop(0, count // step, one, 0)
    if count % step:
        body(count - count % step, count % step)


def gather_face(face, source, target):
    def body(base, size):
        for j in range(size):
            target[pair(2 * (base + j)), :] = source[pair(2 * face[base + j]), :]

    some_rows(face.shape[0], 64, body)


def store_face(face, source, target):
    def body(base, size):
        for j in range(size):
            target[pair(2 * face[base + j]), :] = source[pair(2 * (base + j)), :]

    some_rows(face.shape[0], 64, body)


def add_face(face, source, target):
    def body(base, size):
        places = [pair(2 * face[base + j]) for j in range(size)]
        rows = [target[place, :] for place in places]
        for j in range(size):
            target[places[j], :] = rows[j] + source[pair(2 * (base + j)), :]

    some_rows(face.shape[0], BATCH, body)


def prepare_kernel(width, chunks, face, states, nodes, send, picked, held, sems):
    owned = states.shape[1]
    block = block_of(owned)
    piece = owned // chunks
    copies = []
    for k in range(chunks):
        part = pl.ds(k * piece, piece)
        copies.append(pltpu.make_async_copy(states.at[:, part], held.at[:, part], sems.at[k]))
        copies[-1].start()
    unit = identity(block)
    for k in range(chunks):
        copies[k].wait()

        def one(i, _):
            first = pl.multiple_of(k * piece + i * block, block)
            turned = across(unit, padded_rows(held[:, pl.ds(first, block)]))
            low, high = node_rows(first, block)
            nodes[low, :] = turned[:, :LANES]
            nodes[high, :] = turned[:, LANES:]
            return 0

        lax.fori_loop(0, piece // block, one, 0, unroll=True)
    gather_face(face, nodes, picked)
    count = face.shape[0]
    low, high = pack(picked[pl.ds(0, count, 2), :], picked[pl.ds(1, count, 2), :], width)
    send[:count, :] = low.astype(jnp.bfloat16)
    send[count:, :] = high.astype(jnp.bfloat16)


def gather_own(sizes, table, nodes, matrix, values_out, partial, buffers):
    cells, early, early_rows, late_rows, stride = sizes
    for buffer in buffers:
        buffer[...] = jnp.zeros(buffer.shape, jnp.float32)

    def fetch(cell, buffer):
        mine = table.at[pl.ds(cell * stride, stride)]
        for a in range(early):
            buffer[pl.ds(2 * a, 2), :] = nodes[pair(mine[a]), :]

    def finish(cell, buffer):
        low = buffer[pl.ds(0, early_rows, 2), :]
        high = buffer[pl.ds(1, early_rows, 2), :]
        values = jnp.concatenate([low, high], axis=1).astype(jnp.bfloat16)
        values_out[pl.ds(pl.multiple_of(cell * early_rows, early_rows), early_rows), :] = values
        partial[pl.ds(pl.multiple_of(cell * late_rows, late_rows), late_rows), :] = jnp.dot(
            matrix[early_rows:, :early_rows], values, preferred_element_type=jnp.float32
        )

    def two(i, _):
        fetch(2 * i, buffers[0])
        finish(jnp.maximum(2 * i - 1, 0), buffers[1])
        fetch(2 * i + 1, buffers[1])
        finish(2 * i, buffers[0])
        return 0

    lax.fori_loop(0, cells // 2, two, 0)
    finish(cells - 1, buffers[1])


def own_kernel(sizes, regular, table, nodes, matrix, values_out, partial, *buffers):
    @pl.when(regular[0] == 1)
    def _():
        gather_own(sizes, table, nodes, matrix, values_out, partial, buffers)


def own_again_kernel(sizes, regular, face, table, total, picked, matrix, nodes, values_out, partial, *buffers):
    block = 2 * block_of(nodes.shape[0] // 2)

    def one(i, _):
        at = pl.ds(pl.multiple_of(i * block, block), block)
        nodes[at, :] = (total[at, :] / cheb_half).astype(jnp.bfloat16).astype(jnp.float32)
        return 0

    lax.fori_loop(0, nodes.shape[0] // block, one, 0)
    store_face(face, picked, nodes)

    @pl.when(regular[0] == 1)
    def _():
        gather_own(sizes, table, nodes, matrix, values_out, partial, buffers)


def any_cell(sizes, cell, table, nodes, ghosts, matrix, gathered, products):
    cells, early, early_rows, late_rows, stride = sizes
    owned2 = nodes.shape[0]

    def fetch(a, _):
        place = table[cell * stride + a]
        own = nodes[pair(jnp.minimum(place, owned2 - 2)), :]
        other = ghosts[pair(jnp.maximum(place - owned2, 0)), :]
        row = jnp.where(a < early, a, a - early + early_rows)
        gathered[pair(2 * row), :] = jnp.where(place < owned2, own, other)
        return 0

    def multiply():
        rows = early_rows + late_rows
        values = jnp.concatenate(
            [gathered[pl.ds(0, rows, 2), :], gathered[pl.ds(1, rows, 2), :]], axis=1
        ).astype(jnp.bfloat16)
        result = jnp.dot(matrix[...], values, preferred_element_type=jnp.float32)
        products[pl.ds(0, rows, 2), :] = result[:, :LANES]
        products[pl.ds(1, rows, 2), :] = result[:, LANES:]

    return fetch, multiply


def any_cells(sizes, slots, owned_part, table, nodes, ghosts, matrix, gathered, products, total):
    cells, early, early_rows, late_rows, stride = sizes
    owned2 = nodes.shape[0]
    gathered[...] = jnp.zeros(gathered.shape, jnp.float32)

    def one(cell, _):
        fetch, multiply = any_cell(sizes, cell, table, nodes, ghosts, matrix, gathered, products)
        lax.fori_loop(0, slots, fetch, 0)
        multiply()

        def give(a, _):
            place = table[cell * stride + a]
            row = jnp.where(a < early, a, a - early + early_rows)

            @pl.when((place < owned2) == owned_part)
            def _():
                at = pair(place if owned_part else place - owned2)
                total[at, :] = total[at, :] + products[pair(2 * row), :]

            return 0

        lax.fori_loop(0, slots, give, 0)
        return 0

    lax.fori_loop(0, cells, one, 0)


def shared_kernel(sizes, slots, width, regular, table, late_table, arrived, nodes, matrix, partial,
                  send, values_out, ghosts, total, other, gathered, products, any_gathered, any_products):
    cells, early, early_rows, late_rows, stride = sizes
    late = slots - early
    count = ghosts.shape[0] // 2
    low, high = unpack(arrived[...].astype(jnp.float32), count, width)
    ghosts[pl.ds(0, count, 2), :] = low
    ghosts[pl.ds(1, count, 2), :] = high
    total[...] = jnp.zeros(total.shape, jnp.float32)
    other[...] = jnp.zeros(other.shape, jnp.float32)

    @pl.when(regular[0] == 1)
    def _():
        group = 4

        def fetch(i, _):
            for cell in (2 * i, 2 * i + 1):
                mine = late_table.at[pl.ds(cell * LANES, LANES)]
                here = gathered.at[pl.ds(pl.multiple_of(cell * 2 * late_rows, 2 * late_rows), 2 * late_rows)]
                for a in range(late):
                    here[pl.ds(2 * a, 2), :] = ghosts[pair(mine[a]), :]
                here[pl.ds(2 * late, 2 * (late_rows - late)), :] = jnp.zeros(
                    (2 * (late_rows - late), LANES), jnp.float32
                )
            return 0

        lax.fori_loop(0, cells // 2, fetch, 0)

        def multiply(some, _):
            for j in range(group):
                cell = some * group + j
                base = pl.multiple_of(cell * 2 * late_rows, 2 * late_rows)
                here = gathered.at[pl.ds(base, 2 * late_rows)]
                out = products.at[pl.ds(base, 2 * late_rows)]
                values = jnp.concatenate(
                    [here[pl.ds(0, late_rows, 2), :], here[pl.ds(1, late_rows, 2), :]], axis=1
                ).astype(jnp.bfloat16)
                rows = pl.ds(pl.multiple_of(cell * late_rows, late_rows), late_rows)
                values_out[rows, :] = values
                result = partial[rows, :] + jnp.dot(
                    matrix[early_rows:, early_rows:], values, preferred_element_type=jnp.float32
                )
                out[pl.ds(0, late_rows, 2), :] = result[:, :LANES]
                out[pl.ds(1, late_rows, 2), :] = result[:, LANES:]
            return 0

        lax.fori_loop(0, cells // group, multiply, 0)

        def give(i, _):
            two = (2 * i, 2 * i + 1)
            lists = [late_table.at[pl.ds(cell * LANES, LANES)] for cell in two]
            parts = [
                products.at[pl.ds(pl.multiple_of(cell * 2 * late_rows, 2 * late_rows), 2 * late_rows)] for cell in two
            ]
            scatter_rows(lists, late, parts, (total, other))
            return 0

        lax.fori_loop(0, cells // 2, give, 0)

    @pl.when(regular[0] != 1)
    def _():
        any_cells(sizes, slots, False, table, nodes, ghosts, matrix, any_gathered, any_products, total)

    low, high = (total[pl.ds(k, count, 2), :] + other[pl.ds(k, count, 2), :] for k in range(2))
    low, high = pack(low, high, width)
    send[:count, :] = low
    send[count:, :] = high


def scatter_rows(lists, slots, products, totals):
    def start(k, begin):
        size = min(BATCH, slots - begin)
        places = [pair(lists[k][begin + j]) for j in range(size)]
        held = [totals[k][place, :] for place in places]

        def end():
            for j in range(size):
                totals[k][places[j], :] = held[j] + products[k][pl.ds(2 * (begin + j), 2), :]

        return end

    waiting = []
    for begin in range(0, slots, BATCH):
        for k in range(len(totals)):
            waiting.append(start(k, begin))
            if len(waiting) == len(totals):
                waiting.pop(0)()
    for end in waiting:
        end()


def scatter_own(sizes, table, matrix, own_values, late_values, products, totals):
    cells, early, early_rows, late_rows, stride = sizes

    def multiply(cell, product):
        own = own_values[pl.ds(pl.multiple_of(cell * early_rows, early_rows), early_rows), :]
        late = late_values[pl.ds(pl.multiple_of(cell * late_rows, late_rows), late_rows), :]
        values = jnp.concatenate([own, late], axis=0)
        result = jnp.dot(matrix[:early_rows, :], values, preferred_element_type=jnp.float32)
        product[pl.ds(0, early_rows, 2), :] = result[:, :LANES]
        product[pl.ds(1, early_rows, 2), :] = result[:, LANES:]

    def give(cell, pairs):
        lists = [table.at[pl.ds((cell + k) * stride, stride)] for k in range(2)]
        scatter_rows(lists, early, pairs, totals)

    multiply(0, products[0])
    multiply(1, products[1])

    def four(i, _):
        cell = 4 * i
        multiply(cell + 2, products[2])
        multiply(cell + 3, products[3])
        give(cell, products[:2])
        multiply(jnp.minimum(cell + 4, cells - 1), products[0])
        multiply(jnp.minimum(cell + 5, cells - 1), products[1])
        give(cell + 2, products[2:])
        return 0

    lax.fori_loop(0, cells // 4, four, 0)


def factor_kernel(potential, factor):
    owned = factor.shape[0]
    block = block_of(owned)
    unit = identity(block)

    def one(i, _):
        at = pl.ds(pl.multiple_of(i * block, block), block)
        local = jnp.broadcast_to(potential[:, at], (LANES, block))
        factor[at, :] = across_wide(unit, local) - cheb_center
        return 0

    lax.fori_loop(0, owned // block, one, 0, unroll=3)


def scatter_kernel(sizes, slots, width, again, regular, table, factor, matrix, own_values, late_values,
                   arrived, nodes, *rest):
    if again:
        states, total, other, *rest = rest
    else:
        total, other, *rest = rest
    *products, ghosts, any_gathered, any_products = rest
    owned = factor.shape[0]
    block = block_of(owned)

    def begin(i, _):
        first = pl.multiple_of(i * block, block)
        scale = factor[pl.ds(first, block), :]
        for rows in node_rows(first, block):
            value = scale * nodes[rows, :]
            total[rows, :] = value - (cheb_half / 2.0) * states[rows, :] if again else value
        return 0

    lax.fori_loop(0, owned // block, begin, 0)

    @pl.when(regular[0] == 1)
    def _():
        def clear(i, _):
            other[pl.ds(pl.multiple_of(2 * i * block, 2 * block), 2 * block), :] = jnp.zeros(
                (2 * block, LANES), jnp.float32
            )
            return 0

        lax.fori_loop(0, owned // block, clear, 0)
        scatter_own(sizes, table, matrix, own_values, late_values, products, (total, other))

        def join(i, _):
            at = pl.ds(pl.multiple_of(2 * i * block, 2 * block), 2 * block)
            total[at, :] = total[at, :] + other[at, :]
            return 0

        lax.fori_loop(0, owned // block, join, 0)

    @pl.when(regular[0] != 1)
    def _():
        count = ghosts.shape[0] // 2
        low, high = unpack(arrived[...].astype(jnp.float32), count, width)
        ghosts[pl.ds(0, count, 2), :] = low
        ghosts[pl.ds(1, count, 2), :] = high
        any_cells(sizes, slots, True, table, nodes, ghosts, matrix, any_gathered, any_products, total)


def once_kernel(width, face, total, returned, send, picked):
    count = face.shape[0]
    gather_face(face, total, picked)
    low, high = unpack(returned[...], count, width)
    low = ((picked[pl.ds(0, count, 2), :] + low) / cheb_half).astype(jnp.bfloat16)
    high = ((picked[pl.ds(1, count, 2), :] + high) / cheb_half).astype(jnp.bfloat16)
    picked[pl.ds(0, count, 2), :] = low.astype(jnp.float32)
    picked[pl.ds(1, count, 2), :] = high.astype(jnp.float32)
    low, high = pack(low.astype(jnp.float32), high.astype(jnp.float32), width)
    send[:count, :] = low.astype(jnp.bfloat16)
    send[count:, :] = high.astype(jnp.bfloat16)


def twice_kernel(width, face, total_in, returned, total, filtered, spread):
    owned = filtered.shape[1]
    count = face.shape[0]
    low, high = unpack(returned[...], count, width)
    spread[pl.ds(0, count, 2), :] = low
    spread[pl.ds(1, count, 2), :] = high
    add_face(face, spread, total)
    block = block_of(owned)
    unit = identity(2 * LANES)

    def one(i, _):
        first = pl.multiple_of(i * block, block)
        low, high = node_rows(first, block)
        values = jnp.concatenate([total[low, :], total[high, :]], axis=1) * (2.0 / cheb_half)
        filtered[:, pl.ds(first, block)] = across(unit, values.astype(jnp.bfloat16))[:width].astype(jnp.bfloat16)
        return 0

    lax.fori_loop(0, owned // block, one, 0, unroll=3)


def gram_own_kernel(own, block):
    block[...] = across(own[...], own[...])


def gram_kernel(width, place, gram, own, other, slabs):
    half = width // 2
    rest = (width - LANES) // 2

    def write(cross):
        slabs[0] = cross[:, :LANES]
        slabs[1] = jnp.concatenate([gram[:half, :half], cross[:, LANES : LANES + rest]], axis=1)
        slabs[2] = jnp.concatenate([gram[:half, half:], cross[:, LANES + rest :]], axis=1)
        slabs[3] = jnp.concatenate([gram[half:, half:], jnp.zeros((half, LANES - half), jnp.float32)], axis=1)

    @pl.when(place[0] == 0)
    def _():
        write(across(own[:half, :], other[...]))

    @pl.when(place[0] != 0)
    def _():
        write(across(other[half:, :], own[...]))


def exchanged(axis, stride, radix, give):
    count = lax.axis_size(axis)

    def partner(index, step):
        here = index // stride % radix
        return index + ((here + step) % radix - here) * stride

    return [
        lax.ppermute(give(step), axis, [(i, partner(i, step)) for i in range(count)]) for step in range(1, radix)
    ]


def summed_over(slabs, axis):
    count = lax.axis_size(axis)
    place = lax.axis_index(axis)
    radix = slabs.shape[0]
    radices = [radix]
    left = count // radix
    while left > 1:
        some = 4 if left % 4 == 0 else 2 if left % 2 == 0 else left
        radices.append(some)
        left //= some
    digit = place % radix
    take = lambda step: lax.dynamic_index_in_dim(slabs, (digit + step) % radix, 0, keepdims=False)
    piece = functools.reduce(jnp.add, exchanged(axis, 1, radix, take), take(0))
    stride = radix
    for some in radices[1:]:
        piece = functools.reduce(jnp.add, exchanged(axis, stride, some, lambda step: piece), piece)
        stride *= some
    return [piece] + exchanged(axis, 1, radix, lambda step: piece), digit


def root_kernel(width, where, *refs):
    radix = 4
    mine, theirs = refs[:radix], refs[radix : 2 * radix]
    root, own_slabs, other_slabs = refs[2 * radix :]
    digit = where[0]
    place = where[1]
    for step in range(radix):
        slab = lax.rem(digit + radix - step, radix)
        own_slabs[slab] = mine[step][...]
        other_slabs[slab] = theirs[step][...]
    half = width // 2
    rest = (width - LANES) // 2

    def block_of_states(slabs):
        upper = slabs[2][:, :half]
        top = jnp.concatenate([slabs[1][:, :half], upper], axis=1)
        return jnp.concatenate([top, jnp.concatenate([upper.T, slabs[3][:, :half]], axis=1)], axis=0)

    def cross_rows(slabs):
        return jnp.concatenate([slabs[0], slabs[1][:, half : half + rest], slabs[2][:, half : half + rest]], axis=1)

    first = place == 0
    own_cross, other_cross = cross_rows(own_slabs), cross_rows(other_slabs)
    cross = jnp.concatenate(
        [jnp.where(first, own_cross, other_cross), jnp.where(first, other_cross, own_cross)], axis=0
    )
    turned = cross.T
    above, below = jnp.where(first, cross, turned), jnp.where(first, turned, cross)
    margin = jnp.concatenate(
        [
            jnp.concatenate([block_of_states(own_slabs), above], axis=1),
            jnp.concatenate([below, block_of_states(other_slabs)], axis=1),
        ],
        axis=0,
    )
    total = 2 * width
    rows = lax.broadcasted_iota(jnp.int32, (total, total), 0)
    columns = lax.broadcasted_iota(jnp.int32, (total, total), 1)
    triple = jnp.where(rows == columns, 3.0, 0.0)
    product = functools.partial(jnp.dot, precision=lax.Precision.HIGHEST, preferred_element_type=jnp.float32)
    current = margin / jnp.sqrt(jnp.sum(margin * margin) + epsilon)
    factor = triple - current
    current = 0.5 * product(factor, current)
    inverse = 0.5 * factor
    for iteration in range(1, NS_STEPS - 1):
        factor = triple - product(inverse, current)
        current = 0.5 * product(factor, current)
        inverse = 0.5 * product(factor, inverse)
    factor = triple[:width] - product(inverse[:width], current)
    root[...] = (0.5 * product(factor, inverse)).astype(jnp.bfloat16)


def rotate_kernel(width, root, own, other, result):
    result[...] = jnp.dot(root[:, :width], own[...], preferred_element_type=jnp.float32) + jnp.dot(
        root[:, width:], other[...], preferred_element_type=jnp.float32
    )


def local(states, kinetic, potential, cell_nodes, face_map):
    width, owned = states.shape
    cells, slots = cell_nodes.shape
    count = face_map.shape[0]
    side = round(slots ** (1 / 3))
    late = side * side
    early = slots - late
    early_rows = rounded_up(early, 16)
    late_rows = rounded_up(late, 16)
    rows = early_rows + late_rows
    stride = rounded_up(slots, LANES)
    sizes = (cells, early, early_rows, late_rows, stride)
    packed = count + count // (LANES // (width - LANES))

    regular = jnp.all(cell_nodes[:, :early] < owned) & jnp.all(cell_nodes[:, early:] >= owned)
    regular = (regular & (cells % 4 == 0)).astype(jnp.int32).reshape(1)
    table = jnp.pad(2 * cell_nodes, ((0, 0), (0, stride - slots))).reshape(-1)
    late_table = jnp.pad(2 * (cell_nodes[:, early:] - owned), ((0, 0), (0, LANES - late))).reshape(-1)

    def spaced(array, axis):
        head, tail = jnp.split(array, [early], axis)
        fill = lambda part, size: jnp.pad(
            part, [(0, size - part.shape[k]) if k == axis else (0, 0) for k in range(2)]
        )
        return jnp.concatenate([fill(head, early_rows), fill(tail, late_rows)], axis)

    matrix = spaced(spaced(kinetic, 0), 1)
    lumped = potential[None, :]
    wide = jax.ShapeDtypeStruct((2 * owned, LANES), jnp.float32)
    sent = jax.ShapeDtypeStruct((packed, LANES), jnp.bfloat16)
    sent_wide = jax.ShapeDtypeStruct((packed, LANES), jnp.float32)
    face_rows = jax.ShapeDtypeStruct((2 * count, LANES), jnp.float32)
    own_values = jax.ShapeDtypeStruct((cells * early_rows, 2 * LANES), jnp.bfloat16)
    late_values = jax.ShapeDtypeStruct((cells * late_rows, 2 * LANES), jnp.bfloat16)
    partial = jax.ShapeDtypeStruct((cells * late_rows, 2 * LANES), jnp.float32)
    spread = pltpu.VMEM((2 * count, LANES), jnp.float32)
    pairs_own = pltpu.VMEM((2 * early_rows, LANES), jnp.float32)
    pairs_late = pltpu.VMEM((cells * 2 * late_rows, LANES), jnp.float32)
    pairs_any = pltpu.VMEM((2 * rows, LANES), jnp.float32)

    chunks = 9 if owned % (9 * block_of(owned)) == 0 else 1
    begun, send = called(
        functools.partial(prepare_kernel, width, chunks),
        (wide, sent),
        [SMEM, ANY],
        [spread, pltpu.VMEM((width, owned), jnp.bfloat16), pltpu.SemaphoreType.DMA((chunks,))],
        6,
        20,
    )(face_map, states)

    def shared(arrived, nodes, partial):
        return called(
            functools.partial(shared_kernel, sizes, slots, width),
            (sent_wide, late_values),
            [SMEM, SMEM, SMEM, VMEM, VMEM, VMEM, VMEM],
            [spread, spread, spread, pairs_late, pairs_late, pairs_any, pairs_any],
            6,
            24,
        )(regular, table, late_table, arrived, nodes, matrix, partial)

    (factor,) = called(
        factor_kernel, (jax.ShapeDtypeStruct((owned, LANES), jnp.float32),), [VMEM], [], 3, 8
    )(lumped)

    def scattered(again, values, late, arrived, nodes, *before):
        return called(
            functools.partial(scatter_kernel, sizes, slots, width, again),
            (wide,),
            [SMEM, SMEM] + [VMEM] * (6 + len(before)),
            [pltpu.VMEM((2 * owned, LANES), jnp.float32)] + [pairs_own] * 4 + [spread, pairs_any, pairs_any],
            18,
            20,
        )(regular, table, factor, matrix, values, late, arrived, nodes, *before)[0]

    arrived = passed_along(send, "brick", -1)
    values, part = called(
        functools.partial(own_kernel, sizes),
        (own_values, partial),
        [SMEM, SMEM, VMEM, VMEM],
        [pairs_own, pairs_own],
        10,
        16,
    )(regular, table, begun, matrix)
    back, late_in = shared(arrived, begun, part)
    returned = passed_along(back, "brick", 1)
    total = scattered(False, values, late_in, arrived, begun)
    send, picked = called(
        functools.partial(once_kernel, width),
        (sent, face_rows),
        [SMEM, VMEM, VMEM],
        [],
        3,
        16,
    )(face_map, total, returned)
    arrived = passed_along(send, "brick", -1)
    nodes, values, part = called(
        functools.partial(own_again_kernel, sizes),
        (wide, own_values, partial),
        [SMEM, SMEM, SMEM, VMEM, VMEM, VMEM],
        [pairs_own, pairs_own],
        12,
        20,
    )(regular, face_map, table, total, picked, matrix)
    back, late_in = shared(arrived, nodes, part)
    returned = passed_along(back, "brick", 1)
    total = scattered(True, values, late_in, arrived, nodes, begun)
    _, filtered = called(
        functools.partial(twice_kernel, width),
        (wide, jax.ShapeDtypeStruct((width, owned), jnp.bfloat16)),
        [SMEM, VMEM, VMEM],
        [spread],
        5,
        24,
        input_output_aliases={1: 0},
    )(face_map, total, returned)

    place = lax.axis_index("state")
    other = passed_along(filtered, "state", 1)
    (gram,) = called(
        gram_own_kernel, (jax.ShapeDtypeStruct((width, width), jnp.float32),), [VMEM], [], 1, 16
    )(filtered)
    (slabs,) = called(
        functools.partial(gram_kernel, width),
        (jax.ShapeDtypeStruct((4, width // 2, LANES), jnp.float32),),
        [SMEM, VMEM, VMEM, VMEM],
        [],
        1,
        20,
    )(place.astype(jnp.int32).reshape(1), gram, filtered, other)
    mine, digit = summed_over(slabs, "brick")
    theirs = [passed_along(piece, "state", 1) for piece in mine]
    slabs_held = pltpu.VMEM((4, width // 2, LANES), jnp.float32)
    (root,) = called(
        functools.partial(root_kernel, width),
        (jax.ShapeDtypeStruct((width, 2 * width), jnp.bfloat16),),
        [SMEM] + [VMEM] * 8,
        [slabs_held, slabs_held],
        6,
        20,
    )(jnp.stack([digit, place]).astype(jnp.int32), *mine, *theirs)
    block = owned // chunks
    columns = pl.BlockSpec((width, block), lambda i: (0, i))
    return called(
        functools.partial(rotate_kernel, width),
        jax.ShapeDtypeStruct((width, owned), jnp.float32),
        [pl.BlockSpec((width, 2 * width), lambda i: (0, 0)), columns, columns],
        [],
        3,
        16,
        out_specs=columns,
        grid=(chunks,),
    )(root, filtered, other)


def solution(mesh):
    in_specs = (P("state", "brick"), P(), P("brick"), P("brick", None), P("brick"))
    out_specs = P("state", "brick")
    return jax.shard_map(local, mesh=mesh, in_specs=in_specs, out_specs=out_specs, check_vma=False)
```

```python
import functools
import jax
import jax.numpy as jnp
from jax import lax
from jax.experimental import pallas as pl
from jax.experimental.pallas import tpu as pltpu
from jax.sharding import PartitionSpec as P

NS_STEPS = 3
LANES = 128
BATCH = 8
CODES = 32767.0

cheb_center = 3.0
cheb_half = 7.0
epsilon = 1e-06

VMEM = pl.BlockSpec(memory_space=pltpu.VMEM)
SMEM = pl.BlockSpec(memory_space=pltpu.SMEM)
HBM = pl.BlockSpec(memory_space=pltpu.HBM)


def called(kernel, shapes, in_specs, scratch, microseconds, limit, out_specs=None, **options):
    return pl.pallas_call(
        kernel,
        out_shape=shapes,
        in_specs=in_specs,
        out_specs=out_specs or (VMEM,) * len(shapes),
        scratch_shapes=scratch,
        compiler_params=pltpu.CompilerParams(vmem_limit_bytes=limit << 20),
        cost_estimate=pl.CostEstimate(
            flops=int(microseconds * 4e8), bytes_accessed=int(microseconds * 3e6), transcendentals=0
        ),
        **options,
    )


def passed_along(value, axis, steps):
    count = lax.axis_size(axis)
    pairs = [(source, (source + steps) % count) for source in range(count)]
    return lax.ppermute(value, axis, pairs)


def rounded_up(count, unit):
    return -(-count // unit) * unit


def block_of(count):
    for size in (256, 384, 128):
        if count % size == 0:
            return size
    return count


def identity(size):
    rows = lax.broadcasted_iota(jnp.int32, (size, size), 0)
    columns = lax.broadcasted_iota(jnp.int32, (size, size), 1)
    return (rows == columns).astype(jnp.bfloat16)


def across(left, right):
    return lax.dot_general(left, right, (((1,), (1,)), ((), ())), preferred_element_type=jnp.float32)


def split3(wide):
    first = wide.astype(jnp.bfloat16)
    rest = wide - first.astype(jnp.float32)
    second = rest.astype(jnp.bfloat16)
    return first, second, (rest - second.astype(jnp.float32)).astype(jnp.bfloat16)


def diagonal(high, width):
    row = lax.broadcasted_iota(jnp.int32, (LANES, LANES), 0)
    at = width - LANES
    chosen = jnp.where((row >= at) & (row < at + 3), 1.0, 0.0).astype(jnp.bfloat16)
    return jnp.dot(high.astype(jnp.bfloat16), chosen, preferred_element_type=jnp.float32)


def node_rows(start, count):
    return pl.ds(2 * start, count, 2), pl.ds(2 * start + 1, count, 2)


def pair(row):
    return pl.ds(pl.multiple_of(row, 2), 2)


def pack(low, high, width):
    count = low.shape[0]
    rest = width - LANES
    fold = LANES // rest
    part = count // fold
    return low, jnp.concatenate([high[i * part : (i + 1) * part, :rest] for i in range(fold)], axis=1)


def unpack(packed, count, width):
    rest = width - LANES
    fold = LANES // rest
    low = packed[:count]
    high = jnp.concatenate([packed[count:, i * rest : (i + 1) * rest] for i in range(fold)], axis=0)
    return low, jnp.concatenate([high, jnp.zeros((count, LANES - rest), high.dtype)], axis=1)


def some_rows(count, step, body):
    def one(i, _):
        body(i * step, step)
        return 0

    lax.fori_loop(0, count // step, one, 0)
    if count % step:
        body(count - count % step, count % step)


def gather_face(face, source, target):
    def body(base, size):
        for j in range(size):
            target[pair(2 * (base + j)), :] = source[pair(2 * face[base + j]), :]

    some_rows(face.shape[0], 64, body)


def add_face(face, source, target):
    def body(base, size):
        places = [pair(2 * face[base + j]) for j in range(size)]
        rows = [target[place, :] for place in places]
        for j in range(size):
            target[places[j], :] = rows[j] + source[pair(2 * (base + j)), :]

    some_rows(face.shape[0], 16, body)


def group_of(count):
    for size in (12, 8, 9, 6, 4, 3, 2):
        if count % (8 * size) == 0:
            return size
    return 1


def coded(values):
    count = values.shape[0]
    size = group_of(count)
    grouped = values.reshape(count // (8 * size), size, 8, LANES)
    top = jnp.max(jnp.abs(grouped), axis=1, keepdims=True)
    top = jnp.maximum(top * 1.01, 1e-30).astype(jnp.bfloat16)
    codes = jnp.round(grouped * (CODES / top.astype(jnp.float32)))
    return codes.reshape(count, LANES).astype(jnp.int32).astype(jnp.int16), top.reshape(count // size, LANES)


def decoded(codes, top):
    count = codes.shape[0]
    size = count // top.shape[0]
    grouped = codes.astype(jnp.int32).astype(jnp.float32).reshape(count // (8 * size), size, 8, LANES)
    unit = top.astype(jnp.float32).reshape(count // (8 * size), 1, 8, LANES) / CODES
    return (grouped * unit).reshape(count, LANES)


def tables_kernel(sizes, owned, cell_nodes, kinetic, table, late_table, matrix, regular):
    cells, early, early_rows, late_rows, stride = sizes
    slots = cell_nodes.shape[1]
    late = slots - early
    nodes = cell_nodes[...]
    wide_nodes = jnp.concatenate([2 * nodes, jnp.zeros((cells, stride - slots), jnp.int32)], axis=1)
    per = stride // LANES
    for part in range(per):
        table[pl.ds(part, cells, per), :] = wide_nodes[:, part * LANES : (part + 1) * LANES]
    late_table[:, :late] = 2 * (nodes[:, early:] - owned)
    late_table[:, late:] = jnp.zeros((cells, LANES - late), jnp.int32)
    wide = kinetic[...].astype(jnp.float32)
    wide = jnp.concatenate(
        [
            wide[:, :early],
            jnp.zeros((slots, early_rows - early), jnp.float32),
            wide[:, early:],
            jnp.zeros((slots, late_rows - late), jnp.float32),
        ],
        axis=1,
    )
    columns = wide.shape[1]
    wide = jnp.concatenate(
        [
            wide[:early],
            jnp.zeros((early_rows - early, columns), jnp.float32),
            wide[early:],
            jnp.zeros((late_rows - late, columns), jnp.float32),
        ],
        axis=0,
    )
    matrix[...] = wide.astype(jnp.bfloat16)
    slot = lax.broadcasted_iota(jnp.int32, nodes.shape, 1)
    odd = jnp.where((nodes >= owned) == (slot >= early), 0, 1)
    regular[0] = jnp.where((jnp.max(odd) == 0) & (cells % 4 == 0), 1, 0)


def prepare_kernel(width, chunks, face, potential, states, nodes, send, picked, held, sems):
    owned = states.shape[1]
    block = block_of(owned)
    piece = owned // chunks
    copies = []
    for k in range(chunks):
        part = pl.ds(k * piece, piece)
        copies.append(pltpu.make_async_copy(states.at[:, part], held.at[:, part], sems.at[k]))
        copies[-1].start()
    unit = identity(block)
    for k in range(chunks):
        copies[k].wait()

        def one(i, _):
            first = pl.multiple_of(k * piece + i * block, block)
            at = pl.ds(first, block)
            local = potential[:, at] - cheb_center
            parts = split3(local)
            row = lax.broadcasted_iota(jnp.int32, (2 * LANES - width, block), 0)
            tail = jnp.zeros(row.shape, jnp.float32)
            for place, part in enumerate(parts):
                tail = jnp.where(row == place, part.astype(jnp.float32), tail)
            turned = across(unit, jnp.concatenate([held[:, at], tail.astype(jnp.bfloat16)], axis=0))
            low, high = node_rows(first, block)
            nodes[low, :] = turned[:, :LANES]
            nodes[high, :] = turned[:, LANES:]
            return 0

        lax.fori_loop(0, piece // block, one, 0, unroll=True)
    gather_face(face, nodes, picked)
    count = face.shape[0]
    low, high = pack(picked[pl.ds(0, count, 2), :], picked[pl.ds(1, count, 2), :], width)
    send[:count, :] = low.astype(jnp.bfloat16)
    send[count:, :] = high.astype(jnp.bfloat16)


def gather_own(sizes, again, table, nodes, matrix, values_out, partial, buffers):
    cells, early, early_rows, late_rows, stride = sizes
    for buffer in buffers:
        buffer[...] = jnp.zeros(buffer.shape, jnp.float32)

    def fetch(cell, buffer):
        mine = table.at[pl.ds(cell * stride, stride)]
        for a in range(early):
            buffer[pl.ds(2 * a, 2), :] = nodes[pair(mine[a]), :]

    def finish(cell, buffer):
        low = buffer[pl.ds(0, early_rows, 2), :]
        high = buffer[pl.ds(1, early_rows, 2), :]
        values = once_rounded(jnp.concatenate([low, high], axis=1), again)
        values_out[pl.ds(pl.multiple_of(cell * early_rows, early_rows), early_rows), :] = values
        partial[pl.ds(pl.multiple_of(cell * late_rows, late_rows), late_rows), :] = jnp.dot(
            matrix[early_rows:, :early_rows], values, preferred_element_type=jnp.float32
        )

    def two(i, _):
        fetch(2 * i, buffers[0])
        finish(jnp.maximum(2 * i - 1, 0), buffers[1])
        fetch(2 * i + 1, buffers[1])
        finish(2 * i, buffers[0])
        return 0

    lax.fori_loop(0, cells // 2, two, 0)
    finish(cells - 1, buffers[1])


def once_rounded(summed, again):
    return (summed * (1.0 / cheb_half) if again else summed).astype(jnp.bfloat16)


def own_kernel(sizes, again, regular, table, nodes, matrix, values_out, partial, *buffers):
    @pl.when(regular[0] == 1)
    def _():
        gather_own(sizes, again, table, nodes, matrix, values_out, partial, buffers)


def any_cell(sizes, again, cell, table, nodes, ghosts, matrix, gathered, products):
    cells, early, early_rows, late_rows, stride = sizes
    owned2 = nodes.shape[0]

    def fetch(a, _):
        place = table[cell * stride + a]
        own = once_rounded(nodes[pair(jnp.minimum(place, owned2 - 2)), :], again).astype(jnp.float32)
        other = ghosts[pair(jnp.maximum(place - owned2, 0)), :]
        row = jnp.where(a < early, a, a - early + early_rows)
        gathered[pair(2 * row), :] = jnp.where(place < owned2, own, other)
        return 0

    def multiply():
        rows = early_rows + late_rows
        values = jnp.concatenate(
            [gathered[pl.ds(0, rows, 2), :], gathered[pl.ds(1, rows, 2), :]], axis=1
        ).astype(jnp.bfloat16)
        result = jnp.dot(matrix[...], values, preferred_element_type=jnp.float32)
        products[pl.ds(0, rows, 2), :] = result[:, :LANES]
        products[pl.ds(1, rows, 2), :] = result[:, LANES:]

    return fetch, multiply


def any_cells(sizes, again, slots, owned_part, table, nodes, ghosts, matrix, gathered, products, total):
    cells, early, early_rows, late_rows, stride = sizes
    owned2 = nodes.shape[0]
    gathered[...] = jnp.zeros(gathered.shape, jnp.float32)

    def one(cell, _):
        fetch, multiply = any_cell(sizes, again, cell, table, nodes, ghosts, matrix, gathered, products)
        lax.fori_loop(0, slots, fetch, 0)
        multiply()

        def give(a, _):
            place = table[cell * stride + a]
            row = jnp.where(a < early, a, a - early + early_rows)

            @pl.when((place < owned2) == owned_part)
            def _():
                at = pair(place if owned_part else place - owned2)
                total[at, :] = total[at, :] + products[pair(2 * row), :]

            return 0

        lax.fori_loop(0, slots, give, 0)
        return 0

    lax.fori_loop(0, cells, one, 0)


def shared_kernel(sizes, slots, width, again, regular, table_in, late_table, arrived, nodes, matrix, partial,
                  send, tops, values_out, ghosts, total, other, gathered, products, any_gathered, any_products,
                  table, sem):
    cells, early, early_rows, late_rows, stride = sizes
    late = slots - early
    count = ghosts.shape[0] // 2
    low, high = unpack(arrived[...].astype(jnp.float32), count, width)
    ghosts[pl.ds(0, count, 2), :] = low
    ghosts[pl.ds(1, count, 2), :] = high
    total[...] = jnp.zeros(total.shape, jnp.float32)
    other[...] = jnp.zeros(other.shape, jnp.float32)

    @pl.when(regular[0] == 1)
    def _():
        group = 4

        def fetch(i, _):
            for cell in (2 * i, 2 * i + 1):
                mine = late_table.at[pl.ds(cell * LANES, LANES)]
                here = gathered.at[pl.ds(pl.multiple_of(cell * 2 * late_rows, 2 * late_rows), 2 * late_rows)]
                for a in range(late):
                    here[pl.ds(2 * a, 2), :] = ghosts[pair(mine[a]), :]
                here[pl.ds(2 * late, 2 * (late_rows - late)), :] = jnp.zeros(
                    (2 * (late_rows - late), LANES), jnp.float32
                )
            return 0

        lax.fori_loop(0, cells // 2, fetch, 0)

        def multiply(some, _):
            for j in range(group):
                cell = some * group + j
                base = pl.multiple_of(cell * 2 * late_rows, 2 * late_rows)
                here = gathered.at[pl.ds(base, 2 * late_rows)]
                out = products.at[pl.ds(base, 2 * late_rows)]
                values = jnp.concatenate(
                    [here[pl.ds(0, late_rows, 2), :], here[pl.ds(1, late_rows, 2), :]], axis=1
                ).astype(jnp.bfloat16)
                rows = pl.ds(pl.multiple_of(cell * late_rows, late_rows), late_rows)
                values_out[rows, :] = values
                result = partial[rows, :] + jnp.dot(
                    matrix[early_rows:, early_rows:], values, preferred_element_type=jnp.float32
                )
                out[pl.ds(0, late_rows, 2), :] = result[:, :LANES]
                out[pl.ds(1, late_rows, 2), :] = result[:, LANES:]
            return 0

        lax.fori_loop(0, cells // group, multiply, 0)

        def give(i, _):
            two = (2 * i, 2 * i + 1)
            lists = [late_table.at[pl.ds(cell * LANES, LANES)] for cell in two]
            parts = [
                products.at[pl.ds(pl.multiple_of(cell * 2 * late_rows, 2 * late_rows), 2 * late_rows)] for cell in two
            ]
            scatter_rows(lists, late, parts, (total, other))
            return 0

        lax.fori_loop(0, cells // 2, give, 0)

    @pl.when(regular[0] != 1)
    def _():
        copy = pltpu.make_async_copy(table_in, table, sem)
        copy.start()
        copy.wait()
        any_cells(sizes, again, slots, False, table, nodes, ghosts, matrix, any_gathered, any_products, total)

    low, high = (total[pl.ds(k, count, 2), :] + other[pl.ds(k, count, 2), :] for k in range(2))
    low, high = pack(low, high, width)
    codes, top = coded(jnp.concatenate([low, high], axis=0))
    send[...] = codes
    tops[...] = top


def scatter_rows(lists, slots, products, totals):
    def start(k, begin):
        size = min(BATCH, slots - begin)
        places = [pair(lists[k][begin + j]) for j in range(size)]
        held = [totals[k][place, :] for place in places]

        def end():
            for j in range(size):
                totals[k][places[j], :] = held[j] + products[k][pl.ds(2 * (begin + j), 2), :]

        return end

    waiting = []
    for begin in range(0, slots, BATCH):
        for k in range(len(totals)):
            waiting.append(start(k, begin))
            if len(waiting) == len(totals):
                waiting.pop(0)()
    for end in waiting:
        end()


def scatter_own(sizes, table, matrix, own_values, late_values, products, totals):
    cells, early, early_rows, late_rows, stride = sizes

    def multiply(cell, product):
        own = own_values[pl.ds(pl.multiple_of(cell * early_rows, early_rows), early_rows), :]
        late = late_values[pl.ds(pl.multiple_of(cell * late_rows, late_rows), late_rows), :]
        values = jnp.concatenate([own, late], axis=0)
        result = jnp.dot(matrix[:early_rows, :], values, preferred_element_type=jnp.float32)
        product[pl.ds(0, early_rows, 2), :] = result[:, :LANES]
        product[pl.ds(1, early_rows, 2), :] = result[:, LANES:]

    def give(cell, pairs):
        lists = [table.at[pl.ds((cell + k) * stride, stride)] for k in range(2)]
        scatter_rows(lists, early, pairs, totals)

    multiply(0, products[0])
    multiply(1, products[1])

    def four(i, _):
        cell = 4 * i
        multiply(cell + 2, products[2])
        multiply(cell + 3, products[3])
        give(cell, products[:2])
        multiply(jnp.minimum(cell + 4, cells - 1), products[0])
        multiply(jnp.minimum(cell + 5, cells - 1), products[1])
        give(cell + 2, products[2:])
        return 0

    lax.fori_loop(0, cells // 4, four, 0)


def scatter_kernel(sizes, slots, width, again, regular, table, matrix, own_values, late_values, arrived,
                   nodes, *rest):
    if again:
        states, total, other, *rest = rest
    else:
        total, other, *rest = rest
    *products, ghosts, any_gathered, any_products = rest
    owned = nodes.shape[0] // 2
    block = block_of(owned)

    def begin(i, _):
        low, high = node_rows(pl.multiple_of(i * block, block), block)
        if again:
            factor = diagonal(states[high, :], width)
            for rows in (low, high):
                value = once_rounded(nodes[rows, :], again).astype(jnp.float32)
                total[rows, :] = factor * value - (cheb_half / 2.0) * states[rows, :]
        else:
            factor = diagonal(nodes[high, :], width)
            for rows in (low, high):
                total[rows, :] = factor * nodes[rows, :]
        return 0

    lax.fori_loop(0, owned // block, begin, 0, unroll=3)

    @pl.when(regular[0] == 1)
    def _():
        def clear(i, _):
            other[pl.ds(pl.multiple_of(2 * i * block, 2 * block), 2 * block), :] = jnp.zeros(
                (2 * block, LANES), jnp.float32
            )
            return 0

        lax.fori_loop(0, owned // block, clear, 0)
        scatter_own(sizes, table, matrix, own_values, late_values, products, (total, other))

        def join(i, _):
            at = pl.ds(pl.multiple_of(2 * i * block, 2 * block), 2 * block)
            total[at, :] = total[at, :] + other[at, :]
            return 0

        lax.fori_loop(0, owned // block, join, 0)

    @pl.when(regular[0] != 1)
    def _():
        count = ghosts.shape[0] // 2
        low, high = unpack(arrived[...].astype(jnp.float32), count, width)
        ghosts[pl.ds(0, count, 2), :] = low
        ghosts[pl.ds(1, count, 2), :] = high
        any_cells(sizes, again, slots, True, table, nodes, ghosts, matrix, any_gathered, any_products, total)


def add_returned(width, face, returned, tops, total, spread):
    count = face.shape[0]
    low, high = unpack(decoded(returned[...], tops[...]), count, width)
    spread[pl.ds(0, count, 2), :] = low
    spread[pl.ds(1, count, 2), :] = high
    add_face(face, spread, total)


def once_kernel(width, face, total_in, returned, tops, total, send, spread):
    count = face.shape[0]
    add_returned(width, face, returned, tops, total, spread)
    gather_face(face, total, spread)
    low = once_rounded(spread[pl.ds(0, count, 2), :], True).astype(jnp.float32)
    high = once_rounded(spread[pl.ds(1, count, 2), :], True).astype(jnp.float32)
    low, high = pack(low, high, width)
    send[:count, :] = low.astype(jnp.bfloat16)
    send[count:, :] = high.astype(jnp.bfloat16)


def filter_half(total, filtered, start, width):
    half = filtered.shape[1]
    block = block_of(half)
    unit = identity(2 * LANES)

    def one(i, _):
        first = pl.multiple_of(i * block, block)
        low, high = node_rows(start + first, block)
        values = jnp.concatenate([total[low, :], total[high, :]], axis=1) * (2.0 / cheb_half)
        filtered[:, pl.ds(first, block)] = across(unit, values.astype(jnp.bfloat16))[:width].astype(jnp.bfloat16)
        return 0

    lax.fori_loop(0, half // block, one, 0, unroll=3)


def twice_kernel(width, face, total_in, returned, tops, total, filtered, spread):
    add_returned(width, face, returned, tops, total, spread)
    filter_half(total, filtered, 0, width)


def second_half_kernel(width, total, filtered):
    filter_half(total, filtered, total.shape[0] // 2 - filtered.shape[1], width)


def gram_own_kernel(first, second, block):
    block[...] = across(first[...], first[...]) + across(second[...], second[...])


def cross_rows_of(own, other, write):
    half = own.shape[0] // 2
    place = lax.axis_index("state")

    @pl.when(place == 0)
    def _():
        write(across(own[:half, :], other[...]))

    @pl.when(place != 0)
    def _():
        write(across(other[half:, :], own[...]))


def cross_kernel(own, other, cross):
    def write(value):
        cross[...] = value

    cross_rows_of(own, other, write)


def gram_kernel(width, gram, begun, own, other, *outs):
    *pieces, slabs = outs
    half = width // 2
    rest = (width - LANES) // 2

    def write(value):
        cross = begun[...] + value
        slabs[0] = cross[:, :LANES]
        slabs[1] = jnp.concatenate([gram[:half, :half], cross[:, LANES : LANES + rest]], axis=1)
        slabs[2] = jnp.concatenate([gram[:half, half:], cross[:, LANES + rest :]], axis=1)
        slabs[3] = jnp.concatenate([gram[half:, half:], jnp.zeros((half, LANES - half), jnp.float32)], axis=1)

    cross_rows_of(own, other, write)
    radix = len(pieces)
    digit = lax.rem(lax.axis_index("brick"), radix)
    for step, piece in enumerate(pieces):
        piece[...] = slabs[lax.rem(digit + step, radix)]


def exchanged(axis, stride, radix, give):
    count = lax.axis_size(axis)

    def partner(index, step):
        here = index // stride % radix
        return index + ((here + step) % radix - here) * stride

    return [
        lax.ppermute(give(step), axis, [(i, partner(i, step)) for i in range(count)]) for step in range(1, radix)
    ]


def summed_over(pieces, axis):
    count = lax.axis_size(axis)
    radix = len(pieces)
    radices = []
    left = count // radix
    while left > 1:
        some = 4 if left % 4 == 0 else 2 if left % 2 == 0 else left
        radices.append(some)
        left //= some
    piece = functools.reduce(jnp.add, exchanged(axis, 1, radix, lambda step: pieces[step]), pieces[0])
    stride = radix
    for some in radices:
        piece = functools.reduce(jnp.add, exchanged(axis, stride, some, lambda step: piece), piece)
        stride *= some
    return [piece] + exchanged(axis, 1, radix, lambda step: piece)


def root_kernel(width, *refs):
    radix = 4
    mine, theirs = refs[:radix], refs[radix : 2 * radix]
    root, own_slabs, other_slabs = refs[2 * radix :]
    digit = lax.rem(lax.axis_index("brick"), radix)
    place = lax.axis_index("state")
    for step in range(radix):
        slab = lax.rem(digit + radix - step, radix)
        own_slabs[slab] = mine[step][...]
        other_slabs[slab] = theirs[step][...]
    half = width // 2
    rest = (width - LANES) // 2

    def block_of_states(slabs):
        upper = slabs[2][:, :half]
        top = jnp.concatenate([slabs[1][:, :half], upper], axis=1)
        return jnp.concatenate([top, jnp.concatenate([upper.T, slabs[3][:, :half]], axis=1)], axis=0)

    def cross_rows(slabs):
        return jnp.concatenate([slabs[0], slabs[1][:, half : half + rest], slabs[2][:, half : half + rest]], axis=1)

    first = place == 0
    own_cross, other_cross = cross_rows(own_slabs), cross_rows(other_slabs)
    cross = jnp.concatenate(
        [jnp.where(first, own_cross, other_cross), jnp.where(first, other_cross, own_cross)], axis=0
    )
    turned = cross.T
    above, below = jnp.where(first, cross, turned), jnp.where(first, turned, cross)
    margin = jnp.concatenate(
        [
            jnp.concatenate([block_of_states(own_slabs), above], axis=1),
            jnp.concatenate([below, block_of_states(other_slabs)], axis=1),
        ],
        axis=0,
    )
    total = 2 * width
    rows = lax.broadcasted_iota(jnp.int32, (total, total), 0)
    columns = lax.broadcasted_iota(jnp.int32, (total, total), 1)
    triple = jnp.where(rows == columns, 3.0, 0.0)
    product = functools.partial(jnp.dot, precision=lax.Precision.HIGHEST, preferred_element_type=jnp.float32)
    current = margin / jnp.sqrt(jnp.sum(margin * margin) + epsilon)
    factor = triple - current
    current = 0.5 * product(factor, current)
    inverse = 0.5 * factor
    for iteration in range(1, NS_STEPS - 1):
        factor = triple - product(inverse, current)
        current = 0.5 * product(factor, current)
        inverse = 0.5 * product(factor, inverse)
    factor = triple[:width] - product(inverse[:width], current)
    root[...] = (0.5 * product(factor, inverse)).astype(jnp.bfloat16)


def rotate_kernel(width, pieces, root, first, first_other, second, second_other, result, held, sems):
    half = first.shape[1]
    size = half // pieces
    copies = []
    for k in range(2 * pieces):
        own, other = (first, first_other) if k < pieces else (second, second_other)
        at = pl.ds(k % pieces * size, size)
        if k >= 2:
            copies[k - 2].wait()
        held[k % 2] = jnp.dot(root[:, :width], own[:, at], preferred_element_type=jnp.float32) + jnp.dot(
            root[:, width:], other[:, at], preferred_element_type=jnp.float32
        )
        copies.append(pltpu.make_async_copy(held.at[k % 2], result.at[:, pl.ds(k * size, size)], sems.at[k % 2]))
        copies[k].start()
    for copy in copies[-2:]:
        copy.wait()


def local(states, kinetic, potential, cell_nodes, face_map):
    width, owned = states.shape
    cells, slots = cell_nodes.shape
    count = face_map.shape[0]
    side = round(slots ** (1 / 3))
    late = side * side
    early = slots - late
    early_rows = rounded_up(early, 16)
    late_rows = rounded_up(late, 16)
    rows = early_rows + late_rows
    stride = rounded_up(slots, LANES)
    sizes = (cells, early, early_rows, late_rows, stride)
    packed = count + count // (LANES // (width - LANES))
    integers = lambda *shape: jax.ShapeDtypeStruct(shape, jnp.int32)

    lumped = potential[None, :]
    wide = jax.ShapeDtypeStruct((2 * owned, LANES), jnp.float32)
    sent = jax.ShapeDtypeStruct((packed, LANES), jnp.bfloat16)
    own_values = jax.ShapeDtypeStruct((cells * early_rows, 2 * LANES), jnp.bfloat16)
    late_values = jax.ShapeDtypeStruct((cells * late_rows, 2 * LANES), jnp.bfloat16)
    partial = jax.ShapeDtypeStruct((cells * late_rows, 2 * LANES), jnp.float32)
    spread = pltpu.VMEM((2 * count, LANES), jnp.float32)
    pairs_own = pltpu.VMEM((2 * early_rows, LANES), jnp.float32)
    pairs_late = pltpu.VMEM((cells * 2 * late_rows, LANES), jnp.float32)
    pairs_any = pltpu.VMEM((2 * rows, LANES), jnp.float32)

    chunks = 9 if owned % (9 * block_of(owned)) == 0 else 1
    begun, send = called(
        functools.partial(prepare_kernel, width, chunks),
        (wide, sent),
        [SMEM, VMEM, HBM],
        [spread, pltpu.VMEM((width, owned), jnp.bfloat16), pltpu.SemaphoreType.DMA((chunks,))],
        6,
        6,
    )(face_map, lumped, states)

    table, late_table, matrix, regular = called(
        functools.partial(tables_kernel, sizes, owned),
        (
            integers(cells * (stride // LANES), LANES),
            integers(cells, LANES),
            jax.ShapeDtypeStruct((rows, rows), jnp.bfloat16),
            integers(1),
        ),
        [VMEM, VMEM],
        [],
        2,
        8,
        out_specs=(VMEM, VMEM, VMEM, SMEM),
    )(cell_nodes, kinetic)
    table, late_table = table.reshape(-1), late_table.reshape(-1)
    sent_short = jax.ShapeDtypeStruct((packed, LANES), jnp.int16)
    tops = jax.ShapeDtypeStruct((packed // group_of(packed), LANES), jnp.bfloat16)

    def shared(again, arrived, nodes, partial):
        return called(
            functools.partial(shared_kernel, sizes, slots, width, again),
            (sent_short, tops, late_values),
            [SMEM, VMEM, SMEM, VMEM, VMEM, VMEM, VMEM],
            [spread, spread, spread, pairs_late, pairs_late, pairs_any, pairs_any]
            + [pltpu.SMEM((cells * stride,), jnp.int32), pltpu.SemaphoreType.DMA],
            6,
            11,
        )(regular, table, late_table, arrived, nodes, matrix, partial)

    def own(again, nodes):
        return called(
            functools.partial(own_kernel, sizes, again),
            (own_values, partial),
            [SMEM, SMEM, VMEM, VMEM],
            [pairs_own, pairs_own],
            11,
            3,
        )(regular, table, nodes, matrix)

    def scattered(again, values, late, arrived, nodes, *before):
        return called(
            functools.partial(scatter_kernel, sizes, slots, width, again),
            (wide,),
            [SMEM, SMEM] + [VMEM] * (5 + len(before)),
            [pltpu.VMEM((2 * owned, LANES), jnp.float32)] + [pairs_own] * 4 + [spread, pairs_any, pairs_any],
            18,
            14,
        )(regular, table, matrix, values, late, arrived, nodes, *before)[0]

    def begun_sums(again, send, nodes, *before):
        arrived = passed_along(send, "brick", -1)
        values, part = own(again, nodes)
        back, top, late_in = shared(again, arrived, nodes, part)
        returned = passed_along(back, "brick", 1)
        returned_top = passed_along(top, "brick", 1)
        return scattered(again, values, late_in, arrived, nodes, *before), returned, returned_top

    total, send = called(
        functools.partial(once_kernel, width),
        (wide, sent),
        [SMEM, VMEM, VMEM, VMEM],
        [spread],
        3,
        6,
        input_output_aliases={1: 0},
    )(face_map, *begun_sums(False, send, begun))
    total, returned, returned_top = begun_sums(True, send, total, begun)
    half = jax.ShapeDtypeStruct((width, owned // 2), jnp.bfloat16)
    total, first = called(
        functools.partial(twice_kernel, width),
        (wide, half),
        [SMEM, VMEM, VMEM, VMEM],
        [spread],
        5,
        6,
        input_output_aliases={1: 0},
    )(face_map, total, returned, returned_top)
    first_other = passed_along(first, "state", 1)
    (second,) = called(functools.partial(second_half_kernel, width), (half,), [VMEM], [], 2, 4)(total)
    second_other = passed_along(second, "state", 1)

    (gram,) = called(
        gram_own_kernel, (jax.ShapeDtypeStruct((width, width), jnp.float32),), [VMEM, VMEM], [], 1, 4
    )(first, second)
    (cross,) = called(
        cross_kernel, (jax.ShapeDtypeStruct((width // 2, width), jnp.float32),), [VMEM, VMEM], [], 1, 4
    )(first, first_other)
    slab = jax.ShapeDtypeStruct((width // 2, LANES), jnp.float32)
    slabs_held = pltpu.VMEM((4, width // 2, LANES), jnp.float32)
    pieces = called(functools.partial(gram_kernel, width), (slab,) * 4, [VMEM] * 4, [slabs_held], 1, 4)(
        gram, cross, second, second_other
    )
    mine = summed_over(pieces, "brick")
    theirs = [passed_along(piece, "state", 1) for piece in mine]
    (root,) = called(
        functools.partial(root_kernel, width),
        (jax.ShapeDtypeStruct((width, 2 * width), jnp.bfloat16),),
        [VMEM] * 8,
        [slabs_held, slabs_held],
        6,
        10,
    )(*mine, *theirs)
    pieces = 3 if owned // 2 % (3 * LANES) == 0 else 1
    return called(
        functools.partial(rotate_kernel, width, pieces),
        jax.ShapeDtypeStruct((width, owned), jnp.float32),
        [VMEM] * 5,
        [pltpu.VMEM((2, width, owned // 2 // pieces), jnp.float32), pltpu.SemaphoreType.DMA((2,))],
        3,
        6,
        out_specs=HBM,
    )(root, first, first_other, second, second_other)


def solution(mesh):
    in_specs = (P("state", "brick"), P(), P("brick"), P("brick", None), P("brick"))
    out_specs = P("state", "brick")
    return jax.shard_map(local, mesh=mesh, in_specs=in_specs, out_specs=out_specs, check_vma=False)
```

```python
import functools
import jax
import jax.numpy as jnp
from jax import lax
from jax.experimental import pallas as pl
from jax.experimental.pallas import tpu as pltpu
from jax.sharding import PartitionSpec as P

NS_STEPS = 3
LANES = 128
BATCH = 8
CODES = 32767.0

cheb_center = 3.0
cheb_half = 7.0
epsilon = 1e-06

VMEM = pl.BlockSpec(memory_space=pltpu.VMEM)
SMEM = pl.BlockSpec(memory_space=pltpu.SMEM)
HBM = pl.BlockSpec(memory_space=pltpu.HBM)


def called(kernel, shapes, in_specs, scratch, microseconds, limit, out_specs=None, **options):
    return pl.pallas_call(
        kernel,
        out_shape=shapes,
        in_specs=in_specs,
        out_specs=out_specs or (VMEM,) * len(shapes),
        scratch_shapes=scratch,
        compiler_params=pltpu.CompilerParams(vmem_limit_bytes=limit << 20),
        cost_estimate=pl.CostEstimate(
            flops=int(microseconds * 4e8), bytes_accessed=int(microseconds * 3e6), transcendentals=0
        ),
        **options,
    )


def passed_along(value, axis, steps):
    count = lax.axis_size(axis)
    pairs = [(source, (source + steps) % count) for source in range(count)]
    return lax.ppermute(value, axis, pairs)


def rounded_up(count, unit):
    return -(-count // unit) * unit


def block_of(count):
    for size in (256, 384, 128):
        if count % size == 0:
            return size
    return count


def identity(size):
    rows = lax.broadcasted_iota(jnp.int32, (size, size), 0)
    columns = lax.broadcasted_iota(jnp.int32, (size, size), 1)
    return (rows == columns).astype(jnp.bfloat16)


def across(left, right):
    return lax.dot_general(left, right, (((1,), (1,)), ((), ())), preferred_element_type=jnp.float32)


def split3(wide):
    first = wide.astype(jnp.bfloat16)
    rest = wide - first.astype(jnp.float32)
    second = rest.astype(jnp.bfloat16)
    return first, second, (rest - second.astype(jnp.float32)).astype(jnp.bfloat16)


def diagonal(high, width):
    row = lax.broadcasted_iota(jnp.int32, (LANES, LANES), 0)
    at = width - LANES
    chosen = jnp.where((row >= at) & (row < at + 3), 1.0, 0.0).astype(jnp.bfloat16)
    return jnp.dot(high.astype(jnp.bfloat16), chosen, preferred_element_type=jnp.float32)


def node_rows(start, count):
    return pl.ds(2 * start, count, 2), pl.ds(2 * start + 1, count, 2)


def pair(row):
    return pl.ds(pl.multiple_of(row, 2), 2)


def pack(low, high, width):
    count = low.shape[0]
    rest = width - LANES
    fold = LANES // rest
    part = count // fold
    return low, jnp.concatenate([high[i * part : (i + 1) * part, :rest] for i in range(fold)], axis=1)


def unpack(packed, count, width):
    rest = width - LANES
    fold = LANES // rest
    low = packed[:count]
    high = jnp.concatenate([packed[count:, i * rest : (i + 1) * rest] for i in range(fold)], axis=0)
    return low, jnp.concatenate([high, jnp.zeros((count, LANES - rest), high.dtype)], axis=1)


def some_rows(count, step, body):
    def one(i, _):
        body(i * step, step)
        return 0

    lax.fori_loop(0, count // step, one, 0)
    if count % step:
        body(count - count % step, count % step)


def gather_face(face, source, target):
    def body(base, size):
        for j in range(size):
            target[pair(2 * (base + j)), :] = source[pair(2 * face[base + j]), :]

    some_rows(face.shape[0], 64, body)


def store_face(face, source, target):
    def body(base, size):
        for j in range(size):
            target[pair(2 * face[base + j]), :] = source[pair(2 * (base + j)), :]

    some_rows(face.shape[0], 64, body)


def add_face(face, source, target):
    def body(base, size):
        places = [pair(2 * face[base + j]) for j in range(size)]
        rows = [target[place, :] for place in places]
        for j in range(size):
            target[places[j], :] = rows[j] + source[pair(2 * (base + j)), :]

    some_rows(face.shape[0], 16, body)


def group_of(count):
    for size in (12, 8, 9, 6, 4, 3, 2):
        if count % (8 * size) == 0:
            return size
    return 1


def coded(values):
    count = values.shape[0]
    size = group_of(count)
    grouped = values.reshape(count // (8 * size), size, 8, LANES)
    top = jnp.max(jnp.abs(grouped), axis=1, keepdims=True)
    top = jnp.maximum(top * 1.01, 1e-30).astype(jnp.bfloat16)
    codes = jnp.round(grouped * (CODES / top.astype(jnp.float32)))
    return codes.reshape(count, LANES).astype(jnp.int32).astype(jnp.int16), top.reshape(count // size, LANES)


def decoded(codes, top):
    count = codes.shape[0]
    size = count // top.shape[0]
    grouped = codes.astype(jnp.int32).astype(jnp.float32).reshape(count // (8 * size), size, 8, LANES)
    unit = top.astype(jnp.float32).reshape(count // (8 * size), 1, 8, LANES) / CODES
    return (grouped * unit).reshape(count, LANES)


def tables_kernel(sizes, owned, cell_nodes, kinetic, table, late_table, matrix, regular):
    cells, early, early_rows, late_rows, stride = sizes
    slots = cell_nodes.shape[1]
    late = slots - early
    nodes = cell_nodes[...]
    wide_nodes = jnp.concatenate([2 * nodes, jnp.zeros((cells, stride - slots), jnp.int32)], axis=1)
    per = stride // LANES
    for part in range(per):
        table[pl.ds(part, cells, per), :] = wide_nodes[:, part * LANES : (part + 1) * LANES]
    late_table[:, :late] = 2 * (nodes[:, early:] - owned)
    late_table[:, late:] = jnp.zeros((cells, LANES - late), jnp.int32)
    wide = kinetic[...].astype(jnp.float32)
    wide = jnp.concatenate(
        [
            wide[:, :early],
            jnp.zeros((slots, early_rows - early), jnp.float32),
            wide[:, early:],
            jnp.zeros((slots, late_rows - late), jnp.float32),
        ],
        axis=1,
    )
    columns = wide.shape[1]
    wide = jnp.concatenate(
        [
            wide[:early],
            jnp.zeros((early_rows - early, columns), jnp.float32),
            wide[early:],
            jnp.zeros((late_rows - late, columns), jnp.float32),
        ],
        axis=0,
    )
    matrix[...] = wide.astype(jnp.bfloat16)
    slot = lax.broadcasted_iota(jnp.int32, nodes.shape, 1)
    odd = jnp.where((nodes >= owned) == (slot >= early), 0, 1)
    regular[0] = jnp.where((jnp.max(odd) == 0) & (cells % 8 == 0), 1, 0)


def prepare_kernel(width, chunks, face, potential, states, nodes, send, picked, held, sems):
    owned = states.shape[1]
    block = block_of(owned)
    piece = owned // chunks
    copies = []
    for k in range(chunks):
        part = pl.ds(k * piece, piece)
        copies.append(pltpu.make_async_copy(states.at[:, part], held.at[:, part], sems.at[k]))
        copies[-1].start()
    unit = identity(block)
    for k in range(chunks):
        copies[k].wait()

        def one(i, _):
            first = pl.multiple_of(k * piece + i * block, block)
            at = pl.ds(first, block)
            rows = block // LANES
            local = jnp.concatenate(
                [potential[pl.ds(first // LANES + k, 1), :] for k in range(rows)], axis=1
            ) - cheb_center
            parts = split3(local)
            row = lax.broadcasted_iota(jnp.int32, (2 * LANES - width, block), 0)
            tail = jnp.zeros(row.shape, jnp.float32)
            for place, part in enumerate(parts):
                tail = jnp.where(row == place, part.astype(jnp.float32), tail)
            turned = across(unit, jnp.concatenate([held[:, at], tail.astype(jnp.bfloat16)], axis=0))
            low, high = node_rows(first, block)
            nodes[low, :] = turned[:, :LANES]
            nodes[high, :] = turned[:, LANES:]
            return 0

        lax.fori_loop(0, piece // block, one, 0, unroll=True)
    gather_face(face, nodes, picked)
    count = face.shape[0]
    low, high = pack(picked[pl.ds(0, count, 2), :], picked[pl.ds(1, count, 2), :], width)
    send[:count, :] = low.astype(jnp.bfloat16)
    send[count:, :] = high.astype(jnp.bfloat16)


def gather_own(sizes, again, table_in, nodes, matrix, values_out, partial, table, sems, buffers):
    cells, early, early_rows, late_rows, stride = sizes
    group = len(buffers) // 2
    steps = cells // (2 * group)
    words = 2 * group * stride

    def part_of(step):
        at = pl.ds(pl.multiple_of(step * words, words), words)
        return pltpu.make_async_copy(table_in.at[at], table.at[at], sems.at[step])

    for step in range(steps):
        part_of(step).start()
    for buffer in buffers:
        buffer[pl.ds(2 * early, 2 * (early_rows - early)), :] = jnp.zeros((2 * (early_rows - early), LANES), jnp.float32)

    def fetch(cell, some):
        lists = [table.at[pl.ds((cell + k) * stride, stride)] for k in range(group)]
        for a in range(early):
            for k in range(group):
                some[k][pl.ds(2 * a, 2), :] = nodes[pair(lists[k][a]), :]

    def finish(first, some):
        for k in range(group):
            cell = first + k
            low = some[k][pl.ds(0, early_rows, 2), :]
            high = some[k][pl.ds(1, early_rows, 2), :]
            values = once_rounded(jnp.concatenate([low, high], axis=1), again)
            values_out[pl.ds(pl.multiple_of(cell * early_rows, early_rows), early_rows), :] = values
            partial[pl.ds(pl.multiple_of(cell * late_rows, late_rows), late_rows), :] = jnp.dot(
                matrix[early_rows:, :early_rows], values, preferred_element_type=jnp.float32
            )

    def two(step, _):
        part_of(step).wait()
        cell = 2 * group * step
        fetch(cell, buffers[:group])
        finish(jnp.maximum(cell - group, 0), buffers[group:])
        fetch(cell + group, buffers[group:])
        finish(cell, buffers[:group])
        return 0

    lax.fori_loop(0, steps, two, 0)
    finish(cells - group, buffers[group:])


def once_rounded(summed, again):
    return (summed * (1.0 / cheb_half) if again else summed).astype(jnp.bfloat16)


def own_kernel(sizes, again, regular, table_in, nodes, matrix, values_out, partial, table, sems, *buffers):
    @pl.when(regular[0] == 1)
    def _():
        gather_own(sizes, again, table_in, nodes, matrix, values_out, partial, table, sems, buffers)


def any_cell(sizes, again, cell, table, nodes, ghosts, matrix, gathered, products):
    cells, early, early_rows, late_rows, stride = sizes
    owned2 = nodes.shape[0]

    def fetch(a, _):
        place = table[cell * stride + a]
        own = once_rounded(nodes[pair(jnp.minimum(place, owned2 - 2)), :], again).astype(jnp.float32)
        other = ghosts[pair(jnp.maximum(place - owned2, 0)), :]
        row = jnp.where(a < early, a, a - early + early_rows)
        gathered[pair(2 * row), :] = jnp.where(place < owned2, own, other)
        return 0

    def multiply():
        rows = early_rows + late_rows
        values = jnp.concatenate(
            [gathered[pl.ds(0, rows, 2), :], gathered[pl.ds(1, rows, 2), :]], axis=1
        ).astype(jnp.bfloat16)
        result = jnp.dot(matrix[...], values, preferred_element_type=jnp.float32)
        products[pl.ds(0, rows, 2), :] = result[:, :LANES]
        products[pl.ds(1, rows, 2), :] = result[:, LANES:]

    return fetch, multiply


def any_cells(sizes, again, slots, owned_part, table, nodes, ghosts, matrix, gathered, products, total):
    cells, early, early_rows, late_rows, stride = sizes
    owned2 = nodes.shape[0]
    gathered[...] = jnp.zeros(gathered.shape, jnp.float32)

    def one(cell, _):
        fetch, multiply = any_cell(sizes, again, cell, table, nodes, ghosts, matrix, gathered, products)
        lax.fori_loop(0, slots, fetch, 0)
        multiply()

        def give(a, _):
            place = table[cell * stride + a]
            row = jnp.where(a < early, a, a - early + early_rows)

            @pl.when((place < owned2) == owned_part)
            def _():
                at = pair(place if owned_part else place - owned2)
                total[at, :] = total[at, :] + products[pair(2 * row), :]

            return 0

        lax.fori_loop(0, slots, give, 0)
        return 0

    lax.fori_loop(0, cells, one, 0)


def shared_kernel(sizes, slots, width, again, regular, table_in, late_table, arrived, nodes, matrix, partial,
                  send, tops, values_out, ghosts, total, other, gathered, products, any_gathered, any_products,
                  table, sem):
    cells, early, early_rows, late_rows, stride = sizes
    late = slots - early
    count = ghosts.shape[0] // 2
    low, high = unpack(arrived[...].astype(jnp.float32), count, width)
    ghosts[pl.ds(0, count, 2), :] = low
    ghosts[pl.ds(1, count, 2), :] = high
    total[...] = jnp.zeros(total.shape, jnp.float32)
    other[...] = jnp.zeros(other.shape, jnp.float32)

    @pl.when(regular[0] == 1)
    def _():
        group = 4

        def fetch(i, _):
            four = [4 * i + k for k in range(4)]
            lists = [late_table.at[pl.ds(cell * LANES, LANES)] for cell in four]
            parts = [
                gathered.at[pl.ds(pl.multiple_of(cell * 2 * late_rows, 2 * late_rows), 2 * late_rows)] for cell in four
            ]
            for a in range(late):
                for k in range(4):
                    parts[k][pl.ds(2 * a, 2), :] = ghosts[pair(lists[k][a]), :]
            for k in range(4):
                parts[k][pl.ds(2 * late, 2 * (late_rows - late)), :] = jnp.zeros(
                    (2 * (late_rows - late), LANES), jnp.float32
                )
            return 0

        lax.fori_loop(0, cells // 4, fetch, 0)

        def multiply(some, _):
            for j in range(group):
                cell = some * group + j
                base = pl.multiple_of(cell * 2 * late_rows, 2 * late_rows)
                here = gathered.at[pl.ds(base, 2 * late_rows)]
                out = products.at[pl.ds(base, 2 * late_rows)]
                values = jnp.concatenate(
                    [here[pl.ds(0, late_rows, 2), :], here[pl.ds(1, late_rows, 2), :]], axis=1
                ).astype(jnp.bfloat16)
                rows = pl.ds(pl.multiple_of(cell * late_rows, late_rows), late_rows)
                values_out[rows, :] = values
                result = partial[rows, :] + jnp.dot(
                    matrix[early_rows:, early_rows:], values, preferred_element_type=jnp.float32
                )
                out[pl.ds(0, late_rows, 2), :] = result[:, :LANES]
                out[pl.ds(1, late_rows, 2), :] = result[:, LANES:]
            return 0

        lax.fori_loop(0, cells // group, multiply, 0)

        def give(i, _):
            two = (2 * i, 2 * i + 1)
            lists = [late_table.at[pl.ds(cell * LANES, LANES)] for cell in two]
            parts = [
                products.at[pl.ds(pl.multiple_of(cell * 2 * late_rows, 2 * late_rows), 2 * late_rows)] for cell in two
            ]
            scatter_rows(lists, late, parts, (total, other))
            return 0

        lax.fori_loop(0, cells // 2, give, 0)

    @pl.when(regular[0] != 1)
    def _():
        copy = pltpu.make_async_copy(table_in, table, sem)
        copy.start()
        copy.wait()
        any_cells(sizes, again, slots, False, table, nodes, ghosts, matrix, any_gathered, any_products, total)

    low, high = (total[pl.ds(k, count, 2), :] + other[pl.ds(k, count, 2), :] for k in range(2))
    low, high = pack(low, high, width)
    codes, top = coded(jnp.concatenate([low, high], axis=0))
    send[...] = codes
    tops[...] = top


def scatter_rows(lists, slots, products, totals):
    def start(k, begin):
        size = min(BATCH, slots - begin)
        places = [pair(lists[k][begin + j]) for j in range(size)]
        held = [totals[k][place, :] for place in places]

        def end():
            for j in range(size):
                totals[k][places[j], :] = held[j] + products[k][pl.ds(2 * (begin + j), 2), :]

        return end

    waiting = []
    for begin in range(0, slots, BATCH):
        for k in range(len(totals)):
            waiting.append(start(k, begin))
            if len(waiting) == len(totals):
                waiting.pop(0)()
    for end in waiting:
        end()


def scatter_own(sizes, table, matrix, own_values, late_values, products, totals):
    cells, early, early_rows, late_rows, stride = sizes

    def multiply(cell, product):
        own = own_values[pl.ds(pl.multiple_of(cell * early_rows, early_rows), early_rows), :]
        late = late_values[pl.ds(pl.multiple_of(cell * late_rows, late_rows), late_rows), :]
        values = jnp.concatenate([own, late], axis=0)
        result = jnp.dot(matrix[:early_rows, :], values, preferred_element_type=jnp.float32)
        product[pl.ds(0, early_rows, 2), :] = result[:, :LANES]
        product[pl.ds(1, early_rows, 2), :] = result[:, LANES:]

    def give(cell, pairs):
        lists = [table.at[pl.ds((cell + k) * stride, stride)] for k in range(2)]
        scatter_rows(lists, early, pairs, totals)

    multiply(0, products[0])
    multiply(1, products[1])

    def four(i, _):
        cell = 4 * i
        multiply(cell + 2, products[2])
        multiply(cell + 3, products[3])
        give(cell, products[:2])
        multiply(jnp.minimum(cell + 4, cells - 1), products[0])
        multiply(jnp.minimum(cell + 5, cells - 1), products[1])
        give(cell + 2, products[2:])
        return 0

    lax.fori_loop(0, cells // 4, four, 0)


def scatter_kernel(sizes, slots, width, again, regular, table_in, matrix, own_values, late_values, arrived,
                   nodes, *rest):
    if again:
        states, total, other, *rest = rest
    else:
        total, other, *rest = rest
    *products, ghosts, any_gathered, any_products, table, sem = rest
    copy = pltpu.make_async_copy(table_in, table, sem)
    copy.start()
    owned = nodes.shape[0] // 2
    block = block_of(owned)

    def begin(i, _):
        low, high = node_rows(pl.multiple_of(i * block, block), block)
        if again:
            factor = diagonal(states[high, :], width)
            for rows in (low, high):
                value = once_rounded(nodes[rows, :], again).astype(jnp.float32)
                total[rows, :] = factor * value - (cheb_half / 2.0) * states[rows, :]
        else:
            factor = diagonal(nodes[high, :], width)
            for rows in (low, high):
                total[rows, :] = factor * nodes[rows, :]
        return 0

    lax.fori_loop(0, owned // block, begin, 0, unroll=3)
    copy.wait()

    @pl.when(regular[0] == 1)
    def _():
        def clear(i, _):
            other[pl.ds(pl.multiple_of(2 * i * block, 2 * block), 2 * block), :] = jnp.zeros(
                (2 * block, LANES), jnp.float32
            )
            return 0

        lax.fori_loop(0, owned // block, clear, 0)
        scatter_own(sizes, table, matrix, own_values, late_values, products, (total, other))

        def join(i, _):
            at = pl.ds(pl.multiple_of(2 * i * block, 2 * block), 2 * block)
            total[at, :] = total[at, :] + other[at, :]
            return 0

        lax.fori_loop(0, owned // block, join, 0)

    @pl.when(regular[0] != 1)
    def _():
        count = ghosts.shape[0] // 2
        low, high = unpack(arrived[...].astype(jnp.float32), count, width)
        ghosts[pl.ds(0, count, 2), :] = low
        ghosts[pl.ds(1, count, 2), :] = high
        any_cells(sizes, again, slots, True, table, nodes, ghosts, matrix, any_gathered, any_products, total)


def add_returned(width, face, returned, tops, total, spread):
    count = face.shape[0]
    low, high = unpack(decoded(returned[...], tops[...]), count, width)
    spread[pl.ds(0, count, 2), :] = low
    spread[pl.ds(1, count, 2), :] = high
    add_face(face, spread, total)


def once_kernel(width, face, total_in, returned, tops, total, send, spread):
    count = face.shape[0]
    gather_face(face, total, spread)
    low, high = unpack(decoded(returned[...], tops[...]), count, width)
    low = spread[pl.ds(0, count, 2), :] + low
    high = spread[pl.ds(1, count, 2), :] + high
    spread[pl.ds(0, count, 2), :] = low
    spread[pl.ds(1, count, 2), :] = high
    low, high = pack(once_rounded(low, True).astype(jnp.float32), once_rounded(high, True).astype(jnp.float32), width)
    send[:count, :] = low.astype(jnp.bfloat16)
    send[count:, :] = high.astype(jnp.bfloat16)
    store_face(face, spread, total)


def filter_half(total, filtered, start, width):
    half = filtered.shape[1]
    block = block_of(half)
    unit = identity(2 * LANES)

    def one(i, _):
        first = pl.multiple_of(i * block, block)
        low, high = node_rows(start + first, block)
        values = jnp.concatenate([total[low, :], total[high, :]], axis=1) * (2.0 / cheb_half)
        filtered[:, pl.ds(first, block)] = across(unit, values.astype(jnp.bfloat16))[:width].astype(jnp.bfloat16)
        return 0

    lax.fori_loop(0, half // block, one, 0, unroll=3)


def twice_kernel(width, face, total_in, returned, tops, total, filtered, spread):
    add_returned(width, face, returned, tops, total, spread)
    filter_half(total, filtered, 0, width)


def second_half_kernel(width, total, filtered):
    filter_half(total, filtered, total.shape[0] // 2 - filtered.shape[1], width)


def gram_own_kernel(first, second, block):
    block[...] = across(first[...], first[...]) + across(second[...], second[...])


def cross_rows_of(own, other, write):
    half = own.shape[0] // 2
    place = lax.axis_index("state")

    @pl.when(place == 0)
    def _():
        write(across(own[:half, :], other[...]))

    @pl.when(place != 0)
    def _():
        write(across(other[half:, :], own[...]))


def cross_kernel(own, other, cross):
    def write(value):
        cross[...] = value

    cross_rows_of(own, other, write)


def gram_kernel(width, gram, begun, own, other, *outs):
    *pieces, slabs = outs
    half = width // 2
    rest = (width - LANES) // 2

    def write(value):
        cross = begun[...] + value
        slabs[0] = cross[:, :LANES]
        slabs[1] = jnp.concatenate([gram[:half, :half], cross[:, LANES : LANES + rest]], axis=1)
        slabs[2] = jnp.concatenate([gram[:half, half:], cross[:, LANES + rest :]], axis=1)
        slabs[3] = jnp.concatenate([gram[half:, half:], jnp.zeros((half, LANES - half), jnp.float32)], axis=1)

    cross_rows_of(own, other, write)
    radix = len(pieces)
    digit = lax.rem(lax.axis_index("brick"), radix)
    for step, piece in enumerate(pieces):
        piece[...] = slabs[lax.rem(digit + step, radix)]


def exchanged(axis, stride, radix, give):
    count = lax.axis_size(axis)

    def partner(index, step):
        here = index // stride % radix
        return index + ((here + step) % radix - here) * stride

    return [
        lax.ppermute(give(step), axis, [(i, partner(i, step)) for i in range(count)]) for step in range(1, radix)
    ]


def summed_over(pieces, axis):
    count = lax.axis_size(axis)
    radix = len(pieces)
    radices = []
    left = count // radix
    while left > 1:
        some = 4 if left % 4 == 0 else 2 if left % 2 == 0 else left
        radices.append(some)
        left //= some
    piece = functools.reduce(jnp.add, exchanged(axis, 1, radix, lambda step: pieces[step]), pieces[0])
    stride = radix
    for some in radices:
        piece = functools.reduce(jnp.add, exchanged(axis, stride, some, lambda step: piece), piece)
        stride *= some
    return [piece] + exchanged(axis, 1, radix, lambda step: piece)


def split2(wide):
    first = wide.astype(jnp.bfloat16)
    return first, (wide - first.astype(jnp.float32)).astype(jnp.bfloat16)


def product(left, right):
    return jnp.dot(
        jnp.concatenate([left[0], left[0], left[1]], axis=1),
        jnp.concatenate([right[0], right[1], right[0]], axis=0),
        preferred_element_type=jnp.float32,
    )


def root_kernel(width, *refs):
    radix = 4
    mine, theirs = refs[:radix], refs[radix : 2 * radix]
    root, own_slabs, other_slabs = refs[2 * radix :]
    digit = lax.rem(lax.axis_index("brick"), radix)
    place = lax.axis_index("state")
    for step in range(radix):
        slab = lax.rem(digit + radix - step, radix)
        own_slabs[slab] = mine[step][...]
        other_slabs[slab] = theirs[step][...]
    half = width // 2
    rest = (width - LANES) // 2

    def block_of_states(slabs):
        upper = slabs[2][:, :half]
        top = jnp.concatenate([slabs[1][:, :half], upper], axis=1)
        return jnp.concatenate([top, jnp.concatenate([upper.T, slabs[3][:, :half]], axis=1)], axis=0)

    def cross_rows(slabs):
        return jnp.concatenate([slabs[0], slabs[1][:, half : half + rest], slabs[2][:, half : half + rest]], axis=1)

    first = place == 0
    own_cross, other_cross = cross_rows(own_slabs), cross_rows(other_slabs)
    cross = jnp.concatenate(
        [jnp.where(first, own_cross, other_cross), jnp.where(first, other_cross, own_cross)], axis=0
    )
    turned = cross.T
    above, below = jnp.where(first, cross, turned), jnp.where(first, turned, cross)
    margin = jnp.concatenate(
        [
            jnp.concatenate([block_of_states(own_slabs), above], axis=1),
            jnp.concatenate([below, block_of_states(other_slabs)], axis=1),
        ],
        axis=0,
    )
    total = 2 * width
    rows = lax.broadcasted_iota(jnp.int32, (total, total), 0)
    columns = lax.broadcasted_iota(jnp.int32, (total, total), 1)
    triple = jnp.where(rows == columns, 3.0, 0.0)
    current = margin / jnp.sqrt(jnp.sum(margin * margin) + epsilon)
    factor = triple - current
    current, inverse = 0.5 * product(split2(factor), split2(current)), 0.5 * factor
    for iteration in range(1, NS_STEPS - 1):
        parts = split2(inverse), split2(current)
        factor = split2(triple - product(*parts))
        current, inverse = 0.5 * product(factor, parts[1]), 0.5 * product(factor, parts[0])
    parts = split2(inverse), split2(current)
    factor = triple[:width] - product([part[:width] for part in parts[0]], parts[1])
    root[...] = (0.5 * product(split2(factor), parts[0])).astype(jnp.bfloat16)


def rotate_kernel(width, pieces, root, first, first_other, second, second_other, result, held, sems):
    half = first.shape[1]
    size = half // pieces
    copies = []
    for k in range(2 * pieces):
        own, other = (first, first_other) if k < pieces else (second, second_other)
        at = pl.ds(k % pieces * size, size)
        if k >= 2:
            copies[k - 2].wait()
        held[k % 2] = jnp.dot(root[:, :width], own[:, at], preferred_element_type=jnp.float32) + jnp.dot(
            root[:, width:], other[:, at], preferred_element_type=jnp.float32
        )
        copies.append(pltpu.make_async_copy(held.at[k % 2], result.at[:, pl.ds(k * size, size)], sems.at[k % 2]))
        copies[k].start()
    for copy in copies[-2:]:
        copy.wait()


def local(states, kinetic, potential, cell_nodes, face_map):
    width, owned = states.shape
    cells, slots = cell_nodes.shape
    count = face_map.shape[0]
    side = round(slots ** (1 / 3))
    late = side * side
    early = slots - late
    early_rows = rounded_up(early, 16)
    late_rows = rounded_up(late, 16)
    rows = early_rows + late_rows
    stride = rounded_up(slots, LANES)
    sizes = (cells, early, early_rows, late_rows, stride)
    packed = count + count // (LANES // (width - LANES))
    integers = lambda *shape: jax.ShapeDtypeStruct(shape, jnp.int32)

    lumped = potential.reshape(-1, LANES)
    wide = jax.ShapeDtypeStruct((2 * owned, LANES), jnp.float32)
    sent = jax.ShapeDtypeStruct((packed, LANES), jnp.bfloat16)
    own_values = jax.ShapeDtypeStruct((cells * early_rows, 2 * LANES), jnp.bfloat16)
    late_values = jax.ShapeDtypeStruct((cells * late_rows, 2 * LANES), jnp.bfloat16)
    partial = jax.ShapeDtypeStruct((cells * late_rows, 2 * LANES), jnp.float32)
    spread = pltpu.VMEM((2 * count, LANES), jnp.float32)
    pairs_own = pltpu.VMEM((2 * early_rows, LANES), jnp.float32)
    pairs_late = pltpu.VMEM((cells * 2 * late_rows, LANES), jnp.float32)
    pairs_any = pltpu.VMEM((2 * rows, LANES), jnp.float32)

    chunks = 9 if owned % (9 * block_of(owned)) == 0 else 1
    begun, send = called(
        functools.partial(prepare_kernel, width, chunks),
        (wide, sent),
        [SMEM, VMEM, HBM],
        [spread, pltpu.VMEM((width, owned), jnp.bfloat16), pltpu.SemaphoreType.DMA((chunks,))],
        6,
        6,
    )(face_map, lumped, states)

    table, late_table, matrix, regular = called(
        functools.partial(tables_kernel, sizes, owned),
        (
            integers(cells * (stride // LANES), LANES),
            integers(cells, LANES),
            jax.ShapeDtypeStruct((rows, rows), jnp.bfloat16),
            integers(1),
        ),
        [VMEM, VMEM],
        [],
        2,
        8,
        out_specs=(VMEM, VMEM, VMEM, SMEM),
    )(cell_nodes, kinetic)
    table, late_table = table.reshape(-1), late_table.reshape(-1)
    sent_short = jax.ShapeDtypeStruct((packed, LANES), jnp.int16)
    tops = jax.ShapeDtypeStruct((packed // group_of(packed), LANES), jnp.bfloat16)

    held_table = pltpu.SMEM((cells * stride,), jnp.int32)

    def shared(again, arrived, nodes, partial):
        return called(
            functools.partial(shared_kernel, sizes, slots, width, again),
            (sent_short, tops, late_values),
            [SMEM, VMEM, SMEM, VMEM, VMEM, VMEM, VMEM],
            [spread, spread, spread, pairs_late, pairs_late, pairs_any, pairs_any]
            + [held_table, pltpu.SemaphoreType.DMA],
            6,
            11,
        )(regular, table, late_table, arrived, nodes, matrix, partial)

    def own(again, nodes):
        return called(
            functools.partial(own_kernel, sizes, again),
            (own_values, partial),
            [SMEM, VMEM, VMEM, VMEM],
            [held_table, pltpu.SemaphoreType.DMA((-(-cells // 8),))] + [pairs_own] * 8,
            10,
            4,
        )(regular, table, nodes, matrix)

    def scattered(again, values, late, arrived, nodes, *before):
        return called(
            functools.partial(scatter_kernel, sizes, slots, width, again),
            (wide,),
            [SMEM] + [VMEM] * (6 + len(before)),
            [pltpu.VMEM((2 * owned, LANES), jnp.float32)] + [pairs_own] * 4 + [spread, pairs_any, pairs_any]
            + [held_table, pltpu.SemaphoreType.DMA],
            18,
            14,
        )(regular, table, matrix, values, late, arrived, nodes, *before)[0]

    def begun_sums(again, send, nodes, *before):
        arrived = passed_along(send, "brick", -1)
        values, part = own(again, nodes)
        back, top, late_in = shared(again, arrived, nodes, part)
        returned = passed_along(back, "brick", 1)
        returned_top = passed_along(top, "brick", 1)
        return scattered(again, values, late_in, arrived, nodes, *before), returned, returned_top

    total, send = called(
        functools.partial(once_kernel, width),
        (wide, sent),
        [SMEM, VMEM, VMEM, VMEM],
        [spread],
        3,
        6,
        input_output_aliases={1: 0},
    )(face_map, *begun_sums(False, send, begun))
    total, returned, returned_top = begun_sums(True, send, total, begun)
    half = jax.ShapeDtypeStruct((width, owned // 2), jnp.bfloat16)
    total, first = called(
        functools.partial(twice_kernel, width),
        (wide, half),
        [SMEM, VMEM, VMEM, VMEM],
        [spread],
        5,
        6,
        input_output_aliases={1: 0},
    )(face_map, total, returned, returned_top)
    first_other = passed_along(first, "state", 1)
    (second,) = called(functools.partial(second_half_kernel, width), (half,), [VMEM], [], 2, 4)(total)
    second_other = passed_along(second, "state", 1)

    (gram,) = called(
        gram_own_kernel, (jax.ShapeDtypeStruct((width, width), jnp.float32),), [VMEM, VMEM], [], 1, 4
    )(first, second)
    (cross,) = called(
        cross_kernel, (jax.ShapeDtypeStruct((width // 2, width), jnp.float32),), [VMEM, VMEM], [], 1, 4
    )(first, first_other)
    slab = jax.ShapeDtypeStruct((width // 2, LANES), jnp.float32)
    slabs_held = pltpu.VMEM((4, width // 2, LANES), jnp.float32)
    pieces = called(functools.partial(gram_kernel, width), (slab,) * 4, [VMEM] * 4, [slabs_held], 1, 4)(
        gram, cross, second, second_other
    )
    mine = summed_over(pieces, "brick")
    theirs = [passed_along(piece, "state", 1) for piece in mine]
    (root,) = called(
        functools.partial(root_kernel, width),
        (jax.ShapeDtypeStruct((width, 2 * width), jnp.bfloat16),),
        [VMEM] * 8,
        [slabs_held, slabs_held],
        6,
        10,
    )(*mine, *theirs)
    pieces = 3 if owned // 2 % (3 * LANES) == 0 else 1
    return called(
        functools.partial(rotate_kernel, width, pieces),
        jax.ShapeDtypeStruct((width, owned), jnp.float32),
        [VMEM] * 5,
        [pltpu.VMEM((2, width, owned // 2 // pieces), jnp.float32), pltpu.SemaphoreType.DMA((2,))],
        3,
        6,
        out_specs=HBM,
    )(root, first, first_other, second, second_other)


def solution(mesh):
    in_specs = (P("state", "brick"), P(), P("brick"), P("brick", None), P("brick"))
    out_specs = P("state", "brick")
    return jax.shard_map(local, mesh=mesh, in_specs=in_specs, out_specs=out_specs, check_vma=False)
```

```python
import functools
import jax
import jax.numpy as jnp
from jax import lax
from jax.experimental import pallas as pl
from jax.experimental.pallas import tpu as pltpu
from jax.sharding import PartitionSpec as P

NS_STEPS = 3
LANES = 128
OWN_BATCH = 5
LATE_BATCH = 7
CODES = 32767.0
STEP = 0.0625

cheb_center = 3.0
cheb_half = 7.0
epsilon = 1e-06

VMEM = pl.BlockSpec(memory_space=pltpu.VMEM)
SMEM = pl.BlockSpec(memory_space=pltpu.SMEM)
HBM = pl.BlockSpec(memory_space=pltpu.HBM)


def called(kernel, shapes, in_specs, scratch, microseconds, limit, out_specs=None, **options):
    return pl.pallas_call(
        kernel,
        out_shape=shapes,
        in_specs=in_specs,
        out_specs=out_specs or (VMEM,) * len(shapes),
        scratch_shapes=scratch,
        compiler_params=pltpu.CompilerParams(vmem_limit_bytes=limit << 20),
        cost_estimate=pl.CostEstimate(
            flops=int(microseconds * 4e8), bytes_accessed=int(microseconds * 3e6), transcendentals=0
        ),
        **options,
    )


def passed_along(value, axis, steps):
    count = lax.axis_size(axis)
    pairs = [(source, (source + steps) % count) for source in range(count)]
    return lax.ppermute(value, axis, pairs)


def rounded_up(count, unit):
    return -(-count // unit) * unit


def block_of(count):
    for size in (256, 384, 128):
        if count % size == 0:
            return size
    return count


def identity(size):
    rows = lax.broadcasted_iota(jnp.int32, (size, size), 0)
    columns = lax.broadcasted_iota(jnp.int32, (size, size), 1)
    return (rows == columns).astype(jnp.bfloat16)


def across(left, right):
    return lax.dot_general(left, right, (((1,), (1,)), ((), ())), preferred_element_type=jnp.float32)


def split3(wide):
    first = wide.astype(jnp.bfloat16)
    rest = wide - first.astype(jnp.float32)
    second = rest.astype(jnp.bfloat16)
    return first, second, (rest - second.astype(jnp.float32)).astype(jnp.bfloat16)


def diagonal(high, width):
    row = lax.broadcasted_iota(jnp.int32, (LANES, LANES), 0)
    at = width - LANES
    chosen = jnp.where((row >= at) & (row < at + 3), 1.0, 0.0).astype(jnp.bfloat16)
    return jnp.dot(high.astype(jnp.bfloat16), chosen, preferred_element_type=jnp.float32)


def node_rows(start, count):
    return pl.ds(2 * start, count, 2), pl.ds(2 * start + 1, count, 2)


def pair(row):
    return pl.ds(pl.multiple_of(row, 2), 2)


def pack(low, high, width):
    count = low.shape[0]
    rest = width - LANES
    fold = LANES // rest
    part = count // fold
    return low, jnp.concatenate([high[i * part : (i + 1) * part, :rest] for i in range(fold)], axis=1)


def packed_rows(count, width):
    return count + count // (LANES // (width - LANES))


def unpack(packed, count, width):
    rest = width - LANES
    fold = LANES // rest
    low = packed[:count]
    high = jnp.concatenate([packed[count:, i * rest : (i + 1) * rest] for i in range(fold)], axis=0)
    return low, jnp.concatenate([high, jnp.zeros((count, LANES - rest), high.dtype)], axis=1)


def some_rows(count, step, body):
    def one(i, _):
        body(i * step, step)
        return 0

    lax.fori_loop(0, count // step, one, 0)
    if count % step:
        body(count - count % step, count % step)


def gather_face(face, source, target):
    def body(base, size):
        for j in range(size):
            target[pair(2 * (base + j)), :] = source[pair(2 * face[base + j]), :]

    some_rows(face.shape[0], 64, body)


def store_face(face, source, target):
    def body(base, size):
        for j in range(size):
            target[pair(2 * face[base + j]), :] = source[pair(2 * (base + j)), :]

    some_rows(face.shape[0], 64, body)


def add_face(face, source, target):
    def body(base, size):
        places = [pair(2 * face[base + j]) for j in range(size)]
        rows = [target[place, :] for place in places]
        for j in range(size):
            target[places[j], :] = rows[j] + source[pair(2 * (base + j)), :]

    some_rows(face.shape[0], 16, body)


def group_of(count):
    for size in (12, 8, 9, 6, 4, 3, 2):
        if count % (8 * size) == 0:
            return size
    return 1


def unit_of(steps):
    return jnp.exp(steps * STEP)


def coded(values):
    count = values.shape[0]
    size = group_of(count)
    grouped = values.reshape(count // (8 * size), size, 8, LANES)
    top = jnp.maximum(jnp.max(jnp.abs(grouped), axis=1, keepdims=True), 1e-30)
    steps = jnp.ceil(jnp.log(top * 1.001) / STEP)
    codes = jnp.round(grouped * (CODES / unit_of(steps)))
    codes = jnp.clip(codes, -CODES, CODES).reshape(count, LANES)
    both = jnp.concatenate([codes, steps.reshape(count // size, LANES)], axis=0)
    return both.astype(jnp.int32).astype(jnp.int16)


def decoded(both, count):
    size = group_of(count)
    wide = both.astype(jnp.int32).astype(jnp.float32)
    grouped = wide[:count].reshape(count // (8 * size), size, 8, LANES)
    unit = unit_of(wide[count:]).reshape(count // (8 * size), 1, 8, LANES) / CODES
    return (grouped * unit).reshape(count, LANES)


def tables_kernel(sizes, owned, cell_nodes, kinetic, table, late_table, matrix, regular):
    cells, early, early_rows, late_rows, stride = sizes
    slots = cell_nodes.shape[1]
    late = slots - early
    nodes = cell_nodes[...]
    wide_nodes = jnp.concatenate([2 * nodes, jnp.zeros((cells, stride - slots), jnp.int32)], axis=1)
    per = stride // LANES
    for part in range(per):
        table[pl.ds(part, cells, per), :] = wide_nodes[:, part * LANES : (part + 1) * LANES]
    late_table[:, :late] = 2 * (nodes[:, early:] - owned)
    late_table[:, late:] = jnp.zeros((cells, LANES - late), jnp.int32)
    wide = kinetic[...].astype(jnp.float32)
    wide = jnp.concatenate(
        [
            wide[:, :early],
            jnp.zeros((slots, early_rows - early), jnp.float32),
            wide[:, early:],
            jnp.zeros((slots, late_rows - late), jnp.float32),
        ],
        axis=1,
    )
    columns = wide.shape[1]
    wide = jnp.concatenate(
        [
            wide[:early],
            jnp.zeros((early_rows - early, columns), jnp.float32),
            wide[early:],
            jnp.zeros((late_rows - late, columns), jnp.float32),
        ],
        axis=0,
    )
    matrix[...] = wide.astype(jnp.bfloat16)
    slot = lax.broadcasted_iota(jnp.int32, nodes.shape, 1)
    odd = jnp.where((nodes >= owned) == (slot >= early), 0, 1)
    regular[0] = jnp.where((jnp.max(odd) == 0) & (cells % 8 == 0), 1, 0)


def prepare_kernel(width, chunks, face, potential, states, nodes, send, picked, held, sems):
    owned = states.shape[1]
    block = block_of(owned)
    piece = owned // chunks
    copies = []
    for k in range(chunks):
        part = pl.ds(k * piece, piece)
        copies.append(pltpu.make_async_copy(states.at[:, part], held.at[:, part], sems.at[k]))
        copies[-1].start()
    unit = identity(block)
    for k in range(chunks):
        copies[k].wait()

        def one(i, _):
            first = pl.multiple_of(k * piece + i * block, block)
            at = pl.ds(first, block)
            rows = block // LANES
            local = jnp.concatenate(
                [potential[pl.ds(first // LANES + k, 1), :] for k in range(rows)], axis=1
            ) - cheb_center
            parts = split3(local)
            row = lax.broadcasted_iota(jnp.int32, (2 * LANES - width, block), 0)
            tail = jnp.zeros(row.shape, jnp.float32)
            for place, part in enumerate(parts):
                tail = jnp.where(row == place, part.astype(jnp.float32), tail)
            turned = across(unit, jnp.concatenate([held[:, at], tail.astype(jnp.bfloat16)], axis=0))
            low, high = node_rows(first, block)
            nodes[low, :] = turned[:, :LANES]
            nodes[high, :] = turned[:, LANES:]
            return 0

        lax.fori_loop(0, piece // block, one, 0, unroll=True)
    gather_face(face, nodes, picked)
    count = face.shape[0]
    low, high = pack(picked[pl.ds(0, count, 2), :], picked[pl.ds(1, count, 2), :], width)
    send[:count, :] = low.astype(jnp.bfloat16)
    send[count:, :] = high.astype(jnp.bfloat16)


def gather_own(sizes, again, table_in, nodes, matrix, values_out, partial, table, sems, buffers):
    cells, early, early_rows, late_rows, stride = sizes
    group = len(buffers) // 2
    steps = cells // (2 * group)
    words = 2 * group * stride

    def part_of(step):
        at = pl.ds(pl.multiple_of(step * words, words), words)
        return pltpu.make_async_copy(table_in.at[at], table.at[at], sems.at[step])

    for step in range(steps):
        part_of(step).start()
    for buffer in buffers:
        buffer[pl.ds(2 * early, 2 * (early_rows - early)), :] = jnp.zeros((2 * (early_rows - early), LANES), jnp.float32)

    def fetch(cell, some):
        lists = [table.at[pl.ds((cell + k) * stride, stride)] for k in range(group)]
        for a in range(early):
            for k in range(group):
                some[k][pl.ds(2 * a, 2), :] = nodes[pair(lists[k][a]), :]

    def finish(first, some):
        for k in range(group):
            cell = first + k
            low = some[k][pl.ds(0, early_rows, 2), :]
            high = some[k][pl.ds(1, early_rows, 2), :]
            values = once_rounded(jnp.concatenate([low, high], axis=1), again)
            values_out[pl.ds(pl.multiple_of(cell * early_rows, early_rows), early_rows), :] = values
            partial[pl.ds(pl.multiple_of(cell * late_rows, late_rows), late_rows), :] = jnp.dot(
                matrix[early_rows:, :early_rows], values, preferred_element_type=jnp.float32
            )

    def two(step, _):
        part_of(step).wait()
        cell = 2 * group * step
        fetch(cell, buffers[:group])
        finish(jnp.maximum(cell - group, 0), buffers[group:])
        fetch(cell + group, buffers[group:])
        finish(cell, buffers[:group])
        return 0

    lax.fori_loop(0, steps, two, 0)
    finish(cells - group, buffers[group:])


def once_rounded(summed, again):
    return (summed * (1.0 / cheb_half) if again else summed).astype(jnp.bfloat16)


def own_kernel(sizes, again, regular, table_in, nodes, matrix, values_out, partial, table, sems, *buffers):
    @pl.when(regular[0] == 1)
    def _():
        gather_own(sizes, again, table_in, nodes, matrix, values_out, partial, table, sems, buffers)


def any_cell(sizes, again, cell, table, nodes, ghosts, matrix, gathered, products):
    cells, early, early_rows, late_rows, stride = sizes
    owned2 = nodes.shape[0]

    def fetch(a, _):
        place = table[cell * stride + a]
        own = once_rounded(nodes[pair(jnp.minimum(place, owned2 - 2)), :], again).astype(jnp.float32)
        other = ghosts[pair(jnp.maximum(place - owned2, 0)), :]
        row = jnp.where(a < early, a, a - early + early_rows)
        gathered[pair(2 * row), :] = jnp.where(place < owned2, own, other)
        return 0

    def multiply():
        rows = early_rows + late_rows
        values = jnp.concatenate(
            [gathered[pl.ds(0, rows, 2), :], gathered[pl.ds(1, rows, 2), :]], axis=1
        ).astype(jnp.bfloat16)
        result = jnp.dot(matrix[...], values, preferred_element_type=jnp.float32)
        products[pl.ds(0, rows, 2), :] = result[:, :LANES]
        products[pl.ds(1, rows, 2), :] = result[:, LANES:]

    return fetch, multiply


def any_cells(sizes, again, slots, owned_part, table, nodes, ghosts, matrix, gathered, products, total):
    cells, early, early_rows, late_rows, stride = sizes
    owned2 = nodes.shape[0]
    gathered[...] = jnp.zeros(gathered.shape, jnp.float32)

    def one(cell, _):
        fetch, multiply = any_cell(sizes, again, cell, table, nodes, ghosts, matrix, gathered, products)
        lax.fori_loop(0, slots, fetch, 0)
        multiply()

        def give(a, _):
            place = table[cell * stride + a]
            row = jnp.where(a < early, a, a - early + early_rows)

            @pl.when((place < owned2) == owned_part)
            def _():
                at = pair(place if owned_part else place - owned2)
                total[at, :] = total[at, :] + products[pair(2 * row), :]

            return 0

        lax.fori_loop(0, slots, give, 0)
        return 0

    lax.fori_loop(0, cells, one, 0)


def shared_kernel(sizes, slots, width, again, regular, table_in, late_table, arrived, nodes, matrix, partial,
                  send, values_out, ghosts, total, other, gathered, products, any_gathered, any_products,
                  table, sem):
    cells, early, early_rows, late_rows, stride = sizes
    late = slots - early
    count = ghosts.shape[0] // 2
    low, high = unpack(arrived[...].astype(jnp.float32), count, width)
    ghosts[pl.ds(0, count, 2), :] = low
    ghosts[pl.ds(1, count, 2), :] = high
    total[...] = jnp.zeros(total.shape, jnp.float32)
    other[...] = jnp.zeros(other.shape, jnp.float32)

    @pl.when(regular[0] == 1)
    def _():
        group = 4

        def fetch(i, _):
            four = [4 * i + k for k in range(4)]
            lists = [late_table.at[pl.ds(cell * LANES, LANES)] for cell in four]
            parts = [
                gathered.at[pl.ds(pl.multiple_of(cell * 2 * late_rows, 2 * late_rows), 2 * late_rows)] for cell in four
            ]
            for a in range(late):
                for k in range(4):
                    parts[k][pl.ds(2 * a, 2), :] = ghosts[pair(lists[k][a]), :]
            for k in range(4):
                parts[k][pl.ds(2 * late, 2 * (late_rows - late)), :] = jnp.zeros(
                    (2 * (late_rows - late), LANES), jnp.float32
                )
            return 0

        lax.fori_loop(0, cells // 4, fetch, 0)

        def multiply(some, _):
            for j in range(group):
                cell = some * group + j
                base = pl.multiple_of(cell * 2 * late_rows, 2 * late_rows)
                here = gathered.at[pl.ds(base, 2 * late_rows)]
                out = products.at[pl.ds(base, 2 * late_rows)]
                values = jnp.concatenate(
                    [here[pl.ds(0, late_rows, 2), :], here[pl.ds(1, late_rows, 2), :]], axis=1
                ).astype(jnp.bfloat16)
                rows = pl.ds(pl.multiple_of(cell * late_rows, late_rows), late_rows)
                values_out[rows, :] = values
                result = partial[rows, :] + jnp.dot(
                    matrix[early_rows:, early_rows:], values, preferred_element_type=jnp.float32
                )
                out[pl.ds(0, late_rows, 2), :] = result[:, :LANES]
                out[pl.ds(1, late_rows, 2), :] = result[:, LANES:]
            return 0

        lax.fori_loop(0, cells // group, multiply, 0)

        def give(i, _):
            two = (2 * i, 2 * i + 1)
            lists = [late_table.at[pl.ds(cell * LANES, LANES)] for cell in two]
            parts = [
                products.at[pl.ds(pl.multiple_of(cell * 2 * late_rows, 2 * late_rows), 2 * late_rows)] for cell in two
            ]
            scatter_rows(lists, late, parts, (total, other), LATE_BATCH)
            return 0

        lax.fori_loop(0, cells // 2, give, 0)

    @pl.when(regular[0] != 1)
    def _():
        copy = pltpu.make_async_copy(table_in, table, sem)
        copy.start()
        copy.wait()
        any_cells(sizes, again, slots, False, table, nodes, ghosts, matrix, any_gathered, any_products, total)

    low, high = (total[pl.ds(k, count, 2), :] + other[pl.ds(k, count, 2), :] for k in range(2))
    low, high = pack(low, high, width)
    send[...] = coded(jnp.concatenate([low, high], axis=0))


def scatter_rows(lists, slots, products, totals, batch):
    def start(k, begin):
        size = min(batch, slots - begin)
        places = [pair(lists[k][begin + j]) for j in range(size)]
        held = [totals[k][place, :] for place in places]

        def end():
            for j in range(size):
                totals[k][places[j], :] = held[j] + products[k][pl.ds(2 * (begin + j), 2), :]

        return end

    waiting = []
    for begin in range(0, slots, batch):
        for k in range(len(totals)):
            waiting.append(start(k, begin))
            if len(waiting) == len(totals):
                waiting.pop(0)()
    for end in waiting:
        end()


def scatter_own(sizes, table, matrix, own_values, late_values, products, totals):
    cells, early, early_rows, late_rows, stride = sizes

    def multiply(cell, product):
        own = own_values[pl.ds(pl.multiple_of(cell * early_rows, early_rows), early_rows), :]
        late = late_values[pl.ds(pl.multiple_of(cell * late_rows, late_rows), late_rows), :]
        values = jnp.concatenate([own, late], axis=0)
        result = jnp.dot(matrix[:early_rows, :], values, preferred_element_type=jnp.float32)
        product[pl.ds(0, early_rows, 2), :] = result[:, :LANES]
        product[pl.ds(1, early_rows, 2), :] = result[:, LANES:]

    def give(cell, pairs):
        lists = [table.at[pl.ds((cell + k) * stride, stride)] for k in range(2)]
        scatter_rows(lists, early, pairs, totals, OWN_BATCH)

    multiply(0, products[0])
    multiply(1, products[1])

    def four(i, _):
        cell = 4 * i
        multiply(cell + 2, products[2])
        multiply(cell + 3, products[3])
        give(cell, products[:2])
        multiply(jnp.minimum(cell + 4, cells - 1), products[0])
        multiply(jnp.minimum(cell + 5, cells - 1), products[1])
        give(cell + 2, products[2:])
        return 0

    lax.fori_loop(0, cells // 4, four, 0)


def scatter_kernel(sizes, slots, width, again, regular, table_in, matrix, own_values, late_values, arrived,
                   nodes, *rest):
    if again:
        states, total, other, *rest = rest
    else:
        total, other, *rest = rest
    *products, ghosts, any_gathered, any_products, table, sem = rest
    copy = pltpu.make_async_copy(table_in, table, sem)
    copy.start()
    owned = nodes.shape[0] // 2
    block = block_of(owned)

    def begin(i, _):
        low, high = node_rows(pl.multiple_of(i * block, block), block)
        if again:
            factor = diagonal(states[high, :], width)
            for rows in (low, high):
                value = once_rounded(nodes[rows, :], again).astype(jnp.float32)
                total[rows, :] = factor * value - (cheb_half / 2.0) * states[rows, :]
        else:
            factor = diagonal(nodes[high, :], width)
            for rows in (low, high):
                total[rows, :] = factor * nodes[rows, :]
        return 0

    lax.fori_loop(0, owned // block, begin, 0, unroll=3)
    copy.wait()

    @pl.when(regular[0] == 1)
    def _():
        def clear(i, _):
            other[pl.ds(pl.multiple_of(2 * i * block, 2 * block), 2 * block), :] = jnp.zeros(
                (2 * block, LANES), jnp.float32
            )
            return 0

        lax.fori_loop(0, owned // block, clear, 0)
        scatter_own(sizes, table, matrix, own_values, late_values, products, (total, other))

        def join(i, _):
            at = pl.ds(pl.multiple_of(2 * i * block, 2 * block), 2 * block)
            total[at, :] = total[at, :] + other[at, :]
            return 0

        lax.fori_loop(0, owned // block, join, 0)

    @pl.when(regular[0] != 1)
    def _():
        count = ghosts.shape[0] // 2
        low, high = unpack(arrived[...].astype(jnp.float32), count, width)
        ghosts[pl.ds(0, count, 2), :] = low
        ghosts[pl.ds(1, count, 2), :] = high
        any_cells(sizes, again, slots, True, table, nodes, ghosts, matrix, any_gathered, any_products, total)


def add_returned(width, face, returned, total, spread):
    count = face.shape[0]
    low, high = unpack(decoded(returned[...], packed_rows(count, width)), count, width)
    spread[pl.ds(0, count, 2), :] = low
    spread[pl.ds(1, count, 2), :] = high
    add_face(face, spread, total)


def once_kernel(width, face, total_in, returned, total, send, spread):
    count = face.shape[0]
    gather_face(face, total, spread)
    low, high = unpack(decoded(returned[...], packed_rows(count, width)), count, width)
    low = spread[pl.ds(0, count, 2), :] + low
    high = spread[pl.ds(1, count, 2), :] + high
    spread[pl.ds(0, count, 2), :] = low
    spread[pl.ds(1, count, 2), :] = high
    low, high = pack(once_rounded(low, True).astype(jnp.float32), once_rounded(high, True).astype(jnp.float32), width)
    send[:count, :] = low.astype(jnp.bfloat16)
    send[count:, :] = high.astype(jnp.bfloat16)
    store_face(face, spread, total)


def filter_half(total, filtered, start, width):
    half = filtered.shape[1]
    block = block_of(half)
    unit = identity(2 * LANES)

    def one(i, _):
        first = pl.multiple_of(i * block, block)
        low, high = node_rows(start + first, block)
        values = jnp.concatenate([total[low, :], total[high, :]], axis=1) * (2.0 / cheb_half)
        filtered[:, pl.ds(first, block)] = across(unit, values.astype(jnp.bfloat16))[:width].astype(jnp.bfloat16)
        return 0

    lax.fori_loop(0, half // block, one, 0, unroll=3)


def twice_kernel(width, face, total_in, returned, total, filtered, spread):
    add_returned(width, face, returned, total, spread)
    filter_half(total, filtered, 0, width)


def second_half_kernel(width, total, filtered):
    filter_half(total, filtered, total.shape[0] // 2 - filtered.shape[1], width)


def gram_own_kernel(first, second, block):
    block[...] = across(first[...], first[...]) + across(second[...], second[...])


def cross_rows_of(own, other, write):
    half = own.shape[0] // 2
    place = lax.axis_index("state")

    @pl.when(place == 0)
    def _():
        write(across(own[:half, :], other[...]))

    @pl.when(place != 0)
    def _():
        write(across(other[half:, :], own[...]))


def cross_kernel(own, other, cross):
    def write(value):
        cross[...] = value

    cross_rows_of(own, other, write)


def gram_kernel(width, gram, begun, own, other, *outs):
    *pieces, slabs = outs
    half = width // 2
    rest = (width - LANES) // 2

    def write(value):
        cross = begun[...] + value
        slabs[0] = cross[:, :LANES]
        slabs[1] = jnp.concatenate([gram[:half, :half], cross[:, LANES : LANES + rest]], axis=1)
        slabs[2] = jnp.concatenate([gram[:half, half:], cross[:, LANES + rest :]], axis=1)
        slabs[3] = jnp.concatenate([gram[half:, half:], jnp.zeros((half, LANES - half), jnp.float32)], axis=1)

    cross_rows_of(own, other, write)
    radix = len(pieces)
    digit = lax.rem(lax.axis_index("brick"), radix)
    for step, piece in enumerate(pieces):
        piece[...] = slabs[lax.rem(digit + step, radix)]


def exchanged(axis, stride, radix, give):
    count = lax.axis_size(axis)

    def partner(index, step):
        here = index // stride % radix
        return index + ((here + step) % radix - here) * stride

    return [
        lax.ppermute(give(step), axis, [(i, partner(i, step)) for i in range(count)]) for step in range(1, radix)
    ]


def summed_over(pieces, axis):
    count = lax.axis_size(axis)
    radix = len(pieces)
    radices = []
    left = count // radix
    while left > 1:
        some = 4 if left % 4 == 0 else 2 if left % 2 == 0 else left
        radices.append(some)
        left //= some
    piece = functools.reduce(jnp.add, exchanged(axis, 1, radix, lambda step: pieces[step]), pieces[0])
    stride = radix
    for some in radices:
        piece = functools.reduce(jnp.add, exchanged(axis, stride, some, lambda step: piece), piece)
        stride *= some
    return [piece] + exchanged(axis, 1, radix, lambda step: piece)


def split2(wide):
    first = wide.astype(jnp.bfloat16)
    return first, (wide - first.astype(jnp.float32)).astype(jnp.bfloat16)


def product(left, right):
    return jnp.dot(
        jnp.concatenate([left[0], left[0], left[1]], axis=1),
        jnp.concatenate([right[0], right[1], right[0]], axis=0),
        preferred_element_type=jnp.float32,
    )


def root_kernel(width, *refs):
    radix = 4
    mine, theirs = refs[:radix], refs[radix : 2 * radix]
    root, own_slabs, other_slabs = refs[2 * radix :]
    digit = lax.rem(lax.axis_index("brick"), radix)
    place = lax.axis_index("state")
    for step in range(radix):
        slab = lax.rem(digit + radix - step, radix)
        own_slabs[slab] = mine[step][...]
        other_slabs[slab] = theirs[step][...]
    half = width // 2
    rest = (width - LANES) // 2

    def block_of_states(slabs):
        upper = slabs[2][:, :half]
        top = jnp.concatenate([slabs[1][:, :half], upper], axis=1)
        return jnp.concatenate([top, jnp.concatenate([upper.T, slabs[3][:, :half]], axis=1)], axis=0)

    def cross_rows(slabs):
        return jnp.concatenate([slabs[0], slabs[1][:, half : half + rest], slabs[2][:, half : half + rest]], axis=1)

    first = place == 0
    own_cross, other_cross = cross_rows(own_slabs), cross_rows(other_slabs)
    cross = jnp.concatenate(
        [jnp.where(first, own_cross, other_cross), jnp.where(first, other_cross, own_cross)], axis=0
    )
    turned = cross.T
    above, below = jnp.where(first, cross, turned), jnp.where(first, turned, cross)
    margin = jnp.concatenate(
        [
            jnp.concatenate([block_of_states(own_slabs), above], axis=1),
            jnp.concatenate([below, block_of_states(other_slabs)], axis=1),
        ],
        axis=0,
    )
    total = 2 * width
    rows = lax.broadcasted_iota(jnp.int32, (total, total), 0)
    columns = lax.broadcasted_iota(jnp.int32, (total, total), 1)
    triple = jnp.where(rows == columns, 3.0, 0.0)
    current = margin / jnp.sqrt(jnp.sum(margin * margin) + epsilon)
    factor = triple - current
    current, inverse = 0.5 * product(split2(factor), split2(current)), 0.5 * factor
    for iteration in range(1, NS_STEPS - 1):
        parts = split2(inverse), split2(current)
        factor = split2(triple - product(*parts))
        current, inverse = 0.5 * product(factor, parts[1]), 0.5 * product(factor, parts[0])
    parts = split2(inverse), split2(current)
    factor = triple[:width] - product([part[:width] for part in parts[0]], parts[1])
    root[...] = (0.5 * product(split2(factor), parts[0])).astype(jnp.bfloat16)


def rotate_kernel(width, pieces, root, first, first_other, second, second_other, result, held, sems):
    half = first.shape[1]
    size = half // pieces
    copies = []
    for k in range(2 * pieces):
        own, other = (first, first_other) if k < pieces else (second, second_other)
        at = pl.ds(k % pieces * size, size)
        if k >= 2:
            copies[k - 2].wait()
        held[k % 2] = jnp.dot(root[:, :width], own[:, at], preferred_element_type=jnp.float32) + jnp.dot(
            root[:, width:], other[:, at], preferred_element_type=jnp.float32
        )
        copies.append(pltpu.make_async_copy(held.at[k % 2], result.at[:, pl.ds(k * size, size)], sems.at[k % 2]))
        copies[k].start()
    for copy in copies[-2:]:
        copy.wait()


def local(states, kinetic, potential, cell_nodes, face_map):
    width, owned = states.shape
    cells, slots = cell_nodes.shape
    count = face_map.shape[0]
    side = round(slots ** (1 / 3))
    late = side * side
    early = slots - late
    early_rows = rounded_up(early, 16)
    late_rows = rounded_up(late, 16)
    rows = early_rows + late_rows
    stride = rounded_up(slots, LANES)
    sizes = (cells, early, early_rows, late_rows, stride)
    packed = packed_rows(count, width)
    integers = lambda *shape: jax.ShapeDtypeStruct(shape, jnp.int32)

    lumped = potential.reshape(-1, LANES)
    wide = jax.ShapeDtypeStruct((2 * owned, LANES), jnp.float32)
    sent = jax.ShapeDtypeStruct((packed, LANES), jnp.bfloat16)
    own_values = jax.ShapeDtypeStruct((cells * early_rows, 2 * LANES), jnp.bfloat16)
    late_values = jax.ShapeDtypeStruct((cells * late_rows, 2 * LANES), jnp.bfloat16)
    partial = jax.ShapeDtypeStruct((cells * late_rows, 2 * LANES), jnp.float32)
    spread = pltpu.VMEM((2 * count, LANES), jnp.float32)
    pairs_own = pltpu.VMEM((2 * early_rows, LANES), jnp.float32)
    pairs_late = pltpu.VMEM((cells * 2 * late_rows, LANES), jnp.float32)
    pairs_any = pltpu.VMEM((2 * rows, LANES), jnp.float32)

    chunks = 9 if owned % (9 * block_of(owned)) == 0 else 1
    begun, send = called(
        functools.partial(prepare_kernel, width, chunks),
        (wide, sent),
        [SMEM, VMEM, HBM],
        [spread, pltpu.VMEM((width, owned), jnp.bfloat16), pltpu.SemaphoreType.DMA((chunks,))],
        6,
        6,
    )(face_map, lumped, states)

    table, late_table, matrix, regular = called(
        functools.partial(tables_kernel, sizes, owned),
        (
            integers(cells * (stride // LANES), LANES),
            integers(cells, LANES),
            jax.ShapeDtypeStruct((rows, rows), jnp.bfloat16),
            integers(1),
        ),
        [VMEM, VMEM],
        [],
        2,
        8,
        out_specs=(VMEM, VMEM, VMEM, SMEM),
    )(cell_nodes, kinetic)
    table, late_table = table.reshape(-1), late_table.reshape(-1)
    sent_short = jax.ShapeDtypeStruct((packed + packed // group_of(packed), LANES), jnp.int16)

    held_table = pltpu.SMEM((cells * stride,), jnp.int32)

    def shared(again, arrived, nodes, partial):
        return called(
            functools.partial(shared_kernel, sizes, slots, width, again),
            (sent_short, late_values),
            [SMEM, VMEM, SMEM, VMEM, VMEM, VMEM, VMEM],
            [spread, spread, spread, pairs_late, pairs_late, pairs_any, pairs_any]
            + [held_table, pltpu.SemaphoreType.DMA],
            6,
            11,
        )(regular, table, late_table, arrived, nodes, matrix, partial)

    def own(again, nodes):
        return called(
            functools.partial(own_kernel, sizes, again),
            (own_values, partial),
            [SMEM, VMEM, VMEM, VMEM],
            [held_table, pltpu.SemaphoreType.DMA((-(-cells // 8),))] + [pairs_own] * 8,
            10,
            4,
        )(regular, table, nodes, matrix)

    def scattered(again, values, late, arrived, nodes, *before):
        return called(
            functools.partial(scatter_kernel, sizes, slots, width, again),
            (wide,),
            [SMEM] + [VMEM] * (6 + len(before)),
            [pltpu.VMEM((2 * owned, LANES), jnp.float32)] + [pairs_own] * 4 + [spread, pairs_any, pairs_any]
            + [held_table, pltpu.SemaphoreType.DMA],
            18,
            14,
        )(regular, table, matrix, values, late, arrived, nodes, *before)[0]

    def begun_sums(again, send, nodes, *before):
        arrived = passed_along(send, "brick", -1)
        values, part = own(again, nodes)
        back, late_in = shared(again, arrived, nodes, part)
        returned = passed_along(back, "brick", 1)
        return scattered(again, values, late_in, arrived, nodes, *before), returned

    total, send = called(
        functools.partial(once_kernel, width),
        (wide, sent),
        [SMEM, VMEM, VMEM],
        [spread],
        3,
        6,
        input_output_aliases={1: 0},
    )(face_map, *begun_sums(False, send, begun))
    total, returned = begun_sums(True, send, total, begun)
    half = jax.ShapeDtypeStruct((width, owned // 2), jnp.bfloat16)
    total, first = called(
        functools.partial(twice_kernel, width),
        (wide, half),
        [SMEM, VMEM, VMEM],
        [spread],
        5,
        6,
        input_output_aliases={1: 0},
    )(face_map, total, returned)
    first_other = passed_along(first, "state", 1)
    (second,) = called(functools.partial(second_half_kernel, width), (half,), [VMEM], [], 2, 4)(total)
    second_other = passed_along(second, "state", 1)

    (gram,) = called(
        gram_own_kernel, (jax.ShapeDtypeStruct((width, width), jnp.float32),), [VMEM, VMEM], [], 1, 4
    )(first, second)
    (cross,) = called(
        cross_kernel, (jax.ShapeDtypeStruct((width // 2, width), jnp.float32),), [VMEM, VMEM], [], 1, 4
    )(first, first_other)
    slab = jax.ShapeDtypeStruct((width // 2, LANES), jnp.float32)
    slabs_held = pltpu.VMEM((4, width // 2, LANES), jnp.float32)
    pieces = called(functools.partial(gram_kernel, width), (slab,) * 4, [VMEM] * 4, [slabs_held], 1, 4)(
        gram, cross, second, second_other
    )
    mine = summed_over(pieces, "brick")
    theirs = [passed_along(piece, "state", 1) for piece in mine]
    (root,) = called(
        functools.partial(root_kernel, width),
        (jax.ShapeDtypeStruct((width, 2 * width), jnp.bfloat16),),
        [VMEM] * 8,
        [slabs_held, slabs_held],
        6,
        10,
    )(*mine, *theirs)
    pieces = 1
    return called(
        functools.partial(rotate_kernel, width, pieces),
        jax.ShapeDtypeStruct((width, owned), jnp.float32),
        [VMEM] * 5,
        [pltpu.VMEM((2, width, owned // 2 // pieces), jnp.float32), pltpu.SemaphoreType.DMA((2,))],
        3,
        8,
        out_specs=HBM,
    )(root, first, first_other, second, second_other)


def solution(mesh):
    in_specs = (P("state", "brick"), P(), P("brick"), P("brick", None), P("brick"))
    out_specs = P("state", "brick")
    return jax.shard_map(local, mesh=mesh, in_specs=in_specs, out_specs=out_specs, check_vma=False)
```

```python
import functools
import jax
import jax.numpy as jnp
from jax import lax
from jax.experimental import pallas as pl
from jax.experimental.pallas import tpu as pltpu
from jax.sharding import PartitionSpec as P

NS_STEPS = 3
LANES = 128
OWN_BATCH = 5
LATE_BATCH = 7
CODES = 32767.0
STEP = 0.0625

cheb_center = 3.0
cheb_half = 7.0
epsilon = 1e-06

VMEM = pl.BlockSpec(memory_space=pltpu.VMEM)
SMEM = pl.BlockSpec(memory_space=pltpu.SMEM)
HBM = pl.BlockSpec(memory_space=pltpu.HBM)


def called(kernel, shapes, in_specs, scratch, microseconds, limit, out_specs=None, **options):
    return pl.pallas_call(
        kernel,
        out_shape=shapes,
        in_specs=in_specs,
        out_specs=out_specs or (VMEM,) * len(shapes),
        scratch_shapes=scratch,
        compiler_params=pltpu.CompilerParams(vmem_limit_bytes=limit << 20),
        cost_estimate=pl.CostEstimate(
            flops=int(microseconds * 4e8), bytes_accessed=int(microseconds * 3e6), transcendentals=0
        ),
        **options,
    )


def passed_along(value, axis, steps):
    count = lax.axis_size(axis)
    pairs = [(source, (source + steps) % count) for source in range(count)]
    return lax.ppermute(value, axis, pairs)


def rounded_up(count, unit):
    return -(-count // unit) * unit


def block_of(count):
    for size in (256, 384, 128):
        if count % size == 0:
            return size
    return count


def identity(size):
    rows = lax.broadcasted_iota(jnp.int32, (size, size), 0)
    columns = lax.broadcasted_iota(jnp.int32, (size, size), 1)
    return (rows == columns).astype(jnp.bfloat16)


def across(left, right):
    return lax.dot_general(left, right, (((1,), (1,)), ((), ())), preferred_element_type=jnp.float32)


def split3(wide):
    first = wide.astype(jnp.bfloat16)
    rest = wide - first.astype(jnp.float32)
    second = rest.astype(jnp.bfloat16)
    return first, second, (rest - second.astype(jnp.float32)).astype(jnp.bfloat16)


def diagonal(high, width):
    row = lax.broadcasted_iota(jnp.int32, (LANES, LANES), 0)
    at = width - LANES
    chosen = jnp.where((row >= at) & (row < at + 3), 1.0, 0.0).astype(jnp.bfloat16)
    return jnp.dot(high.astype(jnp.bfloat16), chosen, preferred_element_type=jnp.float32)


def node_rows(start, count):
    return pl.ds(2 * start, count, 2), pl.ds(2 * start + 1, count, 2)


def pair(row):
    return pl.ds(pl.multiple_of(row, 2), 2)


def pack(low, high, width):
    count = low.shape[0]
    rest = width - LANES
    fold = LANES // rest
    part = count // fold
    return low, jnp.concatenate([high[i * part : (i + 1) * part, :rest] for i in range(fold)], axis=1)


def packed_rows(count, width):
    return count + count // (LANES // (width - LANES))


def unpack(packed, count, width):
    rest = width - LANES
    fold = LANES // rest
    low = packed[:count]
    high = jnp.concatenate([packed[count:, i * rest : (i + 1) * rest] for i in range(fold)], axis=0)
    return low, jnp.concatenate([high, jnp.zeros((count, LANES - rest), high.dtype)], axis=1)


def some_rows(count, step, body):
    def one(i, _):
        body(i * step, step)
        return 0

    lax.fori_loop(0, count // step, one, 0)
    if count % step:
        body(count - count % step, count % step)


def gather_face(face, source, target):
    def body(base, size):
        for j in range(size):
            target[pair(2 * (base + j)), :] = source[pair(2 * face[base + j]), :]

    some_rows(face.shape[0], 64, body)


def store_face(face, source, target):
    def body(base, size):
        for j in range(size):
            target[pair(2 * face[base + j]), :] = source[pair(2 * (base + j)), :]

    some_rows(face.shape[0], 64, body)


def add_face(face, source, target):
    def body(base, size):
        places = [pair(2 * face[base + j]) for j in range(size)]
        rows = [target[place, :] for place in places]
        for j in range(size):
            target[places[j], :] = rows[j] + source[pair(2 * (base + j)), :]

    some_rows(face.shape[0], 16, body)


def group_of(count):
    for size in (12, 8, 9, 6, 4, 3, 2):
        if count % (8 * size) == 0:
            return size
    return 1


def unit_of(steps):
    return jnp.exp(steps * STEP)


def coded(values):
    count = values.shape[0]
    size = group_of(count)
    grouped = values.reshape(count // (8 * size), size, 8, LANES)
    top = jnp.maximum(jnp.max(jnp.abs(grouped), axis=1, keepdims=True), 1e-30)
    steps = jnp.ceil(jnp.log(top * 1.001) / STEP)
    codes = jnp.round(grouped * (CODES / unit_of(steps)))
    codes = jnp.clip(codes, -CODES, CODES).reshape(count, LANES)
    both = jnp.concatenate([codes, steps.reshape(count // size, LANES)], axis=0)
    return both.astype(jnp.int32).astype(jnp.int16)


def decoded(both, count):
    size = group_of(count)
    wide = both.astype(jnp.int32).astype(jnp.float32)
    grouped = wide[:count].reshape(count // (8 * size), size, 8, LANES)
    unit = unit_of(wide[count:]).reshape(count // (8 * size), 1, 8, LANES) / CODES
    return (grouped * unit).reshape(count, LANES)


def tables_kernel(sizes, owned, cell_nodes, kinetic, table, late_table, matrix, regular):
    cells, early, early_rows, late_rows, stride = sizes
    slots = cell_nodes.shape[1]
    late = slots - early
    nodes = cell_nodes[...]
    wide_nodes = jnp.concatenate([2 * nodes, jnp.zeros((cells, stride - slots), jnp.int32)], axis=1)
    per = stride // LANES
    for part in range(per):
        table[pl.ds(part, cells, per), :] = wide_nodes[:, part * LANES : (part + 1) * LANES]
    late_table[:, :late] = 2 * (nodes[:, early:] - owned)
    late_table[:, late:] = jnp.zeros((cells, LANES - late), jnp.int32)
    wide = kinetic[...].astype(jnp.float32)
    wide = jnp.concatenate(
        [
            wide[:, :early],
            jnp.zeros((slots, early_rows - early), jnp.float32),
            wide[:, early:],
            jnp.zeros((slots, late_rows - late), jnp.float32),
        ],
        axis=1,
    )
    columns = wide.shape[1]
    wide = jnp.concatenate(
        [
            wide[:early],
            jnp.zeros((early_rows - early, columns), jnp.float32),
            wide[early:],
            jnp.zeros((late_rows - late, columns), jnp.float32),
        ],
        axis=0,
    )
    matrix[...] = wide.astype(jnp.bfloat16)
    slot = lax.broadcasted_iota(jnp.int32, nodes.shape, 1)
    odd = jnp.where((nodes >= owned) == (slot >= early), 0, 1)
    regular[0] = jnp.where((jnp.max(odd) == 0) & (cells % 8 == 0), 1, 0)


def prepare_kernel(width, chunks, face, potential, states, nodes, send, picked):
    owned = states.shape[1]
    block = block_of(owned)
    piece = owned // chunks
    unit = identity(block)
    for k in range(chunks):

        def one(i, _):
            first = pl.multiple_of(k * piece + i * block, block)
            at = pl.ds(first, block)
            rows = block // LANES
            local = jnp.concatenate(
                [potential[pl.ds(first // LANES + k, 1), :] for k in range(rows)], axis=1
            ) - cheb_center
            parts = split3(local)
            row = lax.broadcasted_iota(jnp.int32, (2 * LANES - width, block), 0)
            tail = jnp.zeros(row.shape, jnp.float32)
            for place, part in enumerate(parts):
                tail = jnp.where(row == place, part.astype(jnp.float32), tail)
            turned = across(unit, jnp.concatenate([states[:, at], tail.astype(jnp.bfloat16)], axis=0))
            low, high = node_rows(first, block)
            nodes[low, :] = turned[:, :LANES]
            nodes[high, :] = turned[:, LANES:]
            return 0

        lax.fori_loop(0, piece // block, one, 0, unroll=True)
    gather_face(face, nodes, picked)
    count = face.shape[0]
    low, high = pack(picked[pl.ds(0, count, 2), :], picked[pl.ds(1, count, 2), :], width)
    send[:count, :] = low.astype(jnp.bfloat16)
    send[count:, :] = high.astype(jnp.bfloat16)


def gather_own(sizes, again, table_in, nodes, matrix, values_out, partial, table, sems, buffers):
    cells, early, early_rows, late_rows, stride = sizes
    group = len(buffers) // 2
    steps = cells // (2 * group)
    words = 2 * group * stride

    def part_of(step):
        at = pl.ds(pl.multiple_of(step * words, words), words)
        return pltpu.make_async_copy(table_in.at[at], table.at[at], sems.at[step])

    for step in range(steps):
        part_of(step).start()
    for buffer in buffers:
        buffer[pl.ds(2 * early, 2 * (early_rows - early)), :] = jnp.zeros((2 * (early_rows - early), LANES), jnp.float32)

    def fetch(cell, some):
        lists = [table.at[pl.ds((cell + k) * stride, stride)] for k in range(group)]
        for a in range(early):
            for k in range(group):
                some[k][pl.ds(2 * a, 2), :] = nodes[pair(lists[k][a]), :]

    def finish(first, some):
        for k in range(group):
            cell = first + k
            low = some[k][pl.ds(0, early_rows, 2), :]
            high = some[k][pl.ds(1, early_rows, 2), :]
            values = once_rounded(jnp.concatenate([low, high], axis=1), again)
            values_out[pl.ds(pl.multiple_of(cell * early_rows, early_rows), early_rows), :] = values
            partial[pl.ds(pl.multiple_of(cell * late_rows, late_rows), late_rows), :] = jnp.dot(
                matrix[early_rows:, :early_rows], values, preferred_element_type=jnp.float32
            )

    def two(step, _):
        part_of(step).wait()
        cell = 2 * group * step
        fetch(cell, buffers[:group])
        finish(jnp.maximum(cell - group, 0), buffers[group:])
        fetch(cell + group, buffers[group:])
        finish(cell, buffers[:group])
        return 0

    lax.fori_loop(0, steps, two, 0)
    finish(cells - group, buffers[group:])


def once_rounded(summed, again):
    return (summed * (1.0 / cheb_half) if again else summed).astype(jnp.bfloat16)


def own_kernel(sizes, again, regular, table_in, nodes, matrix, values_out, partial, table, sems, *buffers):
    @pl.when(regular[0] == 1)
    def _():
        gather_own(sizes, again, table_in, nodes, matrix, values_out, partial, table, sems, buffers)


def any_cell(sizes, again, cell, table, nodes, ghosts, matrix, gathered, products):
    cells, early, early_rows, late_rows, stride = sizes
    owned2 = nodes.shape[0]

    def fetch(a, _):
        place = table[cell * stride + a]
        own = once_rounded(nodes[pair(jnp.minimum(place, owned2 - 2)), :], again).astype(jnp.float32)
        other = ghosts[pair(jnp.maximum(place - owned2, 0)), :]
        row = jnp.where(a < early, a, a - early + early_rows)
        gathered[pair(2 * row), :] = jnp.where(place < owned2, own, other)
        return 0

    def multiply():
        rows = early_rows + late_rows
        values = jnp.concatenate(
            [gathered[pl.ds(0, rows, 2), :], gathered[pl.ds(1, rows, 2), :]], axis=1
        ).astype(jnp.bfloat16)
        result = jnp.dot(matrix[...], values, preferred_element_type=jnp.float32)
        products[pl.ds(0, rows, 2), :] = result[:, :LANES]
        products[pl.ds(1, rows, 2), :] = result[:, LANES:]

    return fetch, multiply


def any_cells(sizes, again, slots, owned_part, table, nodes, ghosts, matrix, gathered, products, total):
    cells, early, early_rows, late_rows, stride = sizes
    owned2 = nodes.shape[0]
    gathered[...] = jnp.zeros(gathered.shape, jnp.float32)

    def one(cell, _):
        fetch, multiply = any_cell(sizes, again, cell, table, nodes, ghosts, matrix, gathered, products)
        lax.fori_loop(0, slots, fetch, 0)
        multiply()

        def give(a, _):
            place = table[cell * stride + a]
            row = jnp.where(a < early, a, a - early + early_rows)

            @pl.when((place < owned2) == owned_part)
            def _():
                at = pair(place if owned_part else place - owned2)
                total[at, :] = total[at, :] + products[pair(2 * row), :]

            return 0

        lax.fori_loop(0, slots, give, 0)
        return 0

    lax.fori_loop(0, cells, one, 0)


def shared_kernel(sizes, slots, width, again, regular, table_in, late_table, arrived, nodes, matrix, partial,
                  send, values_out, ghosts, total, other, gathered, products, any_gathered, any_products,
                  table, sem):
    cells, early, early_rows, late_rows, stride = sizes
    late = slots - early
    count = ghosts.shape[0] // 2
    low, high = unpack(arrived[...].astype(jnp.float32), count, width)
    ghosts[pl.ds(0, count, 2), :] = low
    ghosts[pl.ds(1, count, 2), :] = high
    total[...] = jnp.zeros(total.shape, jnp.float32)
    other[...] = jnp.zeros(other.shape, jnp.float32)

    @pl.when(regular[0] == 1)
    def _():
        group = 4

        def fetch(i, _):
            four = [4 * i + k for k in range(4)]
            lists = [late_table.at[pl.ds(cell * LANES, LANES)] for cell in four]
            parts = [
                gathered.at[pl.ds(pl.multiple_of(cell * 2 * late_rows, 2 * late_rows), 2 * late_rows)] for cell in four
            ]
            for a in range(late):
                for k in range(4):
                    parts[k][pl.ds(2 * a, 2), :] = ghosts[pair(lists[k][a]), :]
            for k in range(4):
                parts[k][pl.ds(2 * late, 2 * (late_rows - late)), :] = jnp.zeros(
                    (2 * (late_rows - late), LANES), jnp.float32
                )
            return 0

        lax.fori_loop(0, cells // 4, fetch, 0)

        def multiply(some, _):
            for j in range(group):
                cell = some * group + j
                base = pl.multiple_of(cell * 2 * late_rows, 2 * late_rows)
                here = gathered.at[pl.ds(base, 2 * late_rows)]
                out = products.at[pl.ds(base, 2 * late_rows)]
                values = jnp.concatenate(
                    [here[pl.ds(0, late_rows, 2), :], here[pl.ds(1, late_rows, 2), :]], axis=1
                ).astype(jnp.bfloat16)
                rows = pl.ds(pl.multiple_of(cell * late_rows, late_rows), late_rows)
                values_out[rows, :] = values
                result = partial[rows, :] + jnp.dot(
                    matrix[early_rows:, early_rows:], values, preferred_element_type=jnp.float32
                )
                out[pl.ds(0, late_rows, 2), :] = result[:, :LANES]
                out[pl.ds(1, late_rows, 2), :] = result[:, LANES:]
            return 0

        lax.fori_loop(0, cells // group, multiply, 0)

        def give(i, _):
            two = (2 * i, 2 * i + 1)
            lists = [late_table.at[pl.ds(cell * LANES, LANES)] for cell in two]
            parts = [
                products.at[pl.ds(pl.multiple_of(cell * 2 * late_rows, 2 * late_rows), 2 * late_rows)] for cell in two
            ]
            scatter_rows(lists, late, parts, (total, other), LATE_BATCH)
            return 0

        lax.fori_loop(0, cells // 2, give, 0)

    @pl.when(regular[0] != 1)
    def _():
        copy = pltpu.make_async_copy(table_in, table, sem)
        copy.start()
        copy.wait()
        any_cells(sizes, again, slots, False, table, nodes, ghosts, matrix, any_gathered, any_products, total)

    low, high = (total[pl.ds(k, count, 2), :] + other[pl.ds(k, count, 2), :] for k in range(2))
    low, high = pack(low, high, width)
    send[...] = coded(jnp.concatenate([low, high], axis=0))


def scatter_rows(lists, slots, products, totals, batch):
    def start(k, begin):
        size = min(batch, slots - begin)
        places = [pair(lists[k][begin + j]) for j in range(size)]
        held = [totals[k][place, :] for place in places]

        def end():
            for j in range(size):
                totals[k][places[j], :] = held[j] + products[k][pl.ds(2 * (begin + j), 2), :]

        return end

    waiting = []
    for begin in range(0, slots, batch):
        for k in range(len(totals)):
            waiting.append(start(k, begin))
            if len(waiting) == len(totals):
                waiting.pop(0)()
    for end in waiting:
        end()


def scatter_own(sizes, table, matrix, own_values, late_values, products, totals):
    cells, early, early_rows, late_rows, stride = sizes

    def multiply(cell, product):
        own = own_values[pl.ds(pl.multiple_of(cell * early_rows, early_rows), early_rows), :]
        late = late_values[pl.ds(pl.multiple_of(cell * late_rows, late_rows), late_rows), :]
        values = jnp.concatenate([own, late], axis=0)
        result = jnp.dot(matrix[:early_rows, :], values, preferred_element_type=jnp.float32)
        product[pl.ds(0, early_rows, 2), :] = result[:, :LANES]
        product[pl.ds(1, early_rows, 2), :] = result[:, LANES:]

    def give(cell, pairs):
        lists = [table.at[pl.ds((cell + k) * stride, stride)] for k in range(2)]
        scatter_rows(lists, early, pairs, totals, OWN_BATCH)

    multiply(0, products[0])
    multiply(1, products[1])

    def four(i, _):
        cell = 4 * i
        multiply(cell + 2, products[2])
        multiply(cell + 3, products[3])
        give(cell, products[:2])
        multiply(jnp.minimum(cell + 4, cells - 1), products[0])
        multiply(jnp.minimum(cell + 5, cells - 1), products[1])
        give(cell + 2, products[2:])
        return 0

    lax.fori_loop(0, cells // 4, four, 0)


def scatter_kernel(sizes, slots, width, again, regular, table_in, matrix, own_values, late_values, arrived,
                   nodes, *rest):
    if again:
        states, total, other, *rest = rest
    else:
        total, other, *rest = rest
    *products, ghosts, any_gathered, any_products, table, sem = rest
    copy = pltpu.make_async_copy(table_in, table, sem)
    copy.start()
    owned = nodes.shape[0] // 2
    block = block_of(owned)

    def begin(i, _):
        low, high = node_rows(pl.multiple_of(i * block, block), block)
        if again:
            factor = diagonal(states[high, :], width)
            for rows in (low, high):
                value = once_rounded(nodes[rows, :], again).astype(jnp.float32)
                total[rows, :] = factor * value - (cheb_half / 2.0) * states[rows, :]
        else:
            factor = diagonal(nodes[high, :], width)
            for rows in (low, high):
                total[rows, :] = factor * nodes[rows, :]
        return 0

    lax.fori_loop(0, owned // block, begin, 0, unroll=3)
    copy.wait()

    @pl.when(regular[0] == 1)
    def _():
        def clear(i, _):
            other[pl.ds(pl.multiple_of(2 * i * block, 2 * block), 2 * block), :] = jnp.zeros(
                (2 * block, LANES), jnp.float32
            )
            return 0

        lax.fori_loop(0, owned // block, clear, 0)
        scatter_own(sizes, table, matrix, own_values, late_values, products, (total, other))

        def join(i, _):
            at = pl.ds(pl.multiple_of(2 * i * block, 2 * block), 2 * block)
            total[at, :] = total[at, :] + other[at, :]
            return 0

        lax.fori_loop(0, owned // block, join, 0)

    @pl.when(regular[0] != 1)
    def _():
        count = ghosts.shape[0] // 2
        low, high = unpack(arrived[...].astype(jnp.float32), count, width)
        ghosts[pl.ds(0, count, 2), :] = low
        ghosts[pl.ds(1, count, 2), :] = high
        any_cells(sizes, again, slots, True, table, nodes, ghosts, matrix, any_gathered, any_products, total)


def add_returned(width, face, returned, total, spread):
    count = face.shape[0]
    low, high = unpack(decoded(returned[...], packed_rows(count, width)), count, width)
    spread[pl.ds(0, count, 2), :] = low
    spread[pl.ds(1, count, 2), :] = high
    add_face(face, spread, total)


def once_kernel(width, face, total_in, returned, total, send, spread):
    count = face.shape[0]
    gather_face(face, total, spread)
    low, high = unpack(decoded(returned[...], packed_rows(count, width)), count, width)
    low = spread[pl.ds(0, count, 2), :] + low
    high = spread[pl.ds(1, count, 2), :] + high
    spread[pl.ds(0, count, 2), :] = low
    spread[pl.ds(1, count, 2), :] = high
    low, high = pack(once_rounded(low, True).astype(jnp.float32), once_rounded(high, True).astype(jnp.float32), width)
    send[:count, :] = low.astype(jnp.bfloat16)
    send[count:, :] = high.astype(jnp.bfloat16)
    store_face(face, spread, total)


def filter_half(total, filtered, start, width):
    half = filtered.shape[1]
    block = block_of(half)
    unit = identity(2 * LANES)

    def one(i, _):
        first = pl.multiple_of(i * block, block)
        low, high = node_rows(start + first, block)
        values = jnp.concatenate([total[low, :], total[high, :]], axis=1) * (2.0 / cheb_half)
        filtered[:, pl.ds(first, block)] = across(unit, values.astype(jnp.bfloat16))[:width].astype(jnp.bfloat16)
        return 0

    lax.fori_loop(0, half // block, one, 0, unroll=3)


def twice_kernel(width, face, total_in, returned, total, filtered, spread):
    add_returned(width, face, returned, total, spread)
    filter_half(total, filtered, 0, width)


def second_half_kernel(width, total, filtered):
    filter_half(total, filtered, total.shape[0] // 2 - filtered.shape[1], width)


def gram_own_kernel(first, second, block):
    block[...] = across(first[...], first[...]) + across(second[...], second[...])


def cross_rows_of(own, other, write):
    half = own.shape[0] // 2
    place = lax.axis_index("state")

    @pl.when(place == 0)
    def _():
        write(across(own[:half, :], other[...]))

    @pl.when(place != 0)
    def _():
        write(across(other[half:, :], own[...]))


def cross_kernel(own, other, cross):
    def write(value):
        cross[...] = value

    cross_rows_of(own, other, write)


def gram_kernel(width, gram, begun, own, other, *outs):
    *pieces, slabs = outs
    half = width // 2
    rest = (width - LANES) // 2

    def write(value):
        cross = begun[...] + value
        slabs[0] = cross[:, :LANES]
        slabs[1] = jnp.concatenate([gram[:half, :half], cross[:, LANES : LANES + rest]], axis=1)
        slabs[2] = jnp.concatenate([gram[:half, half:], cross[:, LANES + rest :]], axis=1)
        slabs[3] = jnp.concatenate([gram[half:, half:], jnp.zeros((half, LANES - half), jnp.float32)], axis=1)

    cross_rows_of(own, other, write)
    radix = len(pieces)
    digit = lax.rem(lax.axis_index("brick"), radix)
    for step, piece in enumerate(pieces):
        piece[...] = slabs[lax.rem(digit + step, radix)]


def exchanged(axis, stride, radix, give):
    count = lax.axis_size(axis)

    def partner(index, step):
        here = index // stride % radix
        return index + ((here + step) % radix - here) * stride

    return [
        lax.ppermute(give(step), axis, [(i, partner(i, step)) for i in range(count)]) for step in range(1, radix)
    ]


def summed_over(pieces, axis):
    count = lax.axis_size(axis)
    radix = len(pieces)
    radices = []
    left = count // radix
    while left > 1:
        some = 4 if left % 4 == 0 else 2 if left % 2 == 0 else left
        radices.append(some)
        left //= some
    piece = functools.reduce(jnp.add, exchanged(axis, 1, radix, lambda step: pieces[step]), pieces[0])
    stride = radix
    for some in radices:
        piece = functools.reduce(jnp.add, exchanged(axis, stride, some, lambda step: piece), piece)
        stride *= some
    return [piece] + exchanged(axis, 1, radix, lambda step: piece)


def split2(wide):
    first = wide.astype(jnp.bfloat16)
    return first, (wide - first.astype(jnp.float32)).astype(jnp.bfloat16)


def product(left, right):
    return jnp.dot(
        jnp.concatenate([left[0], left[0], left[1]], axis=1),
        jnp.concatenate([right[0], right[1], right[0]], axis=0),
        preferred_element_type=jnp.float32,
    )


def root_kernel(width, *refs):
    radix = 4
    mine, theirs = refs[:radix], refs[radix : 2 * radix]
    root, own_slabs, other_slabs = refs[2 * radix :]
    digit = lax.rem(lax.axis_index("brick"), radix)
    place = lax.axis_index("state")
    for step in range(radix):
        slab = lax.rem(digit + radix - step, radix)
        own_slabs[slab] = mine[step][...]
        other_slabs[slab] = theirs[step][...]
    half = width // 2
    rest = (width - LANES) // 2

    def block_of_states(slabs):
        upper = slabs[2][:, :half]
        top = jnp.concatenate([slabs[1][:, :half], upper], axis=1)
        return jnp.concatenate([top, jnp.concatenate([upper.T, slabs[3][:, :half]], axis=1)], axis=0)

    def cross_rows(slabs):
        return jnp.concatenate([slabs[0], slabs[1][:, half : half + rest], slabs[2][:, half : half + rest]], axis=1)

    first = place == 0
    own_cross, other_cross = cross_rows(own_slabs), cross_rows(other_slabs)
    cross = jnp.concatenate(
        [jnp.where(first, own_cross, other_cross), jnp.where(first, other_cross, own_cross)], axis=0
    )
    turned = cross.T
    above, below = jnp.where(first, cross, turned), jnp.where(first, turned, cross)
    margin = jnp.concatenate(
        [
            jnp.concatenate([block_of_states(own_slabs), above], axis=1),
            jnp.concatenate([below, block_of_states(other_slabs)], axis=1),
        ],
        axis=0,
    )
    total = 2 * width
    rows = lax.broadcasted_iota(jnp.int32, (total, total), 0)
    columns = lax.broadcasted_iota(jnp.int32, (total, total), 1)
    triple = jnp.where(rows == columns, 3.0, 0.0)
    current = margin / jnp.sqrt(jnp.sum(margin * margin) + epsilon)
    factor = triple - current
    current, inverse = 0.5 * product(split2(factor), split2(current)), 0.5 * factor
    for iteration in range(1, NS_STEPS - 1):
        parts = split2(inverse), split2(current)
        factor = split2(triple - product(*parts))
        current, inverse = 0.5 * product(factor, parts[1]), 0.5 * product(factor, parts[0])
    parts = split2(inverse), split2(current)
    factor = triple[:width] - product([part[:width] for part in parts[0]], parts[1])
    root[...] = (0.5 * product(split2(factor), parts[0])).astype(jnp.bfloat16)


def rotate_kernel(width, pieces, root, first, first_other, second, second_other, result, held, sems):
    half = first.shape[1]
    size = half // pieces
    copies = []
    for k in range(2 * pieces):
        own, other = (first, first_other) if k < pieces else (second, second_other)
        at = pl.ds(k % pieces * size, size)
        if k >= 2:
            copies[k - 2].wait()
        held[k % 2] = jnp.dot(root[:, :width], own[:, at], preferred_element_type=jnp.float32) + jnp.dot(
            root[:, width:], other[:, at], preferred_element_type=jnp.float32
        )
        copies.append(pltpu.make_async_copy(held.at[k % 2], result.at[:, pl.ds(k * size, size)], sems.at[k % 2]))
        copies[k].start()
    for copy in copies[-2:]:
        copy.wait()


def local(states, kinetic, potential, cell_nodes, face_map):
    width, owned = states.shape
    cells, slots = cell_nodes.shape
    count = face_map.shape[0]
    side = round(slots ** (1 / 3))
    late = side * side
    early = slots - late
    early_rows = rounded_up(early, 16)
    late_rows = rounded_up(late, 16)
    rows = early_rows + late_rows
    stride = rounded_up(slots, LANES)
    sizes = (cells, early, early_rows, late_rows, stride)
    packed = packed_rows(count, width)
    integers = lambda *shape: jax.ShapeDtypeStruct(shape, jnp.int32)

    lumped = potential.reshape(-1, LANES)
    wide = jax.ShapeDtypeStruct((2 * owned, LANES), jnp.float32)
    sent = jax.ShapeDtypeStruct((packed, LANES), jnp.bfloat16)
    own_values = jax.ShapeDtypeStruct((cells * early_rows, 2 * LANES), jnp.bfloat16)
    late_values = jax.ShapeDtypeStruct((cells * late_rows, 2 * LANES), jnp.bfloat16)
    partial = jax.ShapeDtypeStruct((cells * late_rows, 2 * LANES), jnp.float32)
    spread = pltpu.VMEM((2 * count, LANES), jnp.float32)
    pairs_own = pltpu.VMEM((2 * early_rows, LANES), jnp.float32)
    pairs_late = pltpu.VMEM((cells * 2 * late_rows, LANES), jnp.float32)
    pairs_any = pltpu.VMEM((2 * rows, LANES), jnp.float32)

    chunks = 9 if owned % (9 * block_of(owned)) == 0 else 1
    begun, send = called(
        functools.partial(prepare_kernel, width, chunks),
        (wide, sent),
        [SMEM, VMEM, VMEM],
        [spread],
        6,
        6,
    )(face_map, lumped, states)

    table, late_table, matrix, regular = called(
        functools.partial(tables_kernel, sizes, owned),
        (
            integers(cells * (stride // LANES), LANES),
            integers(cells, LANES),
            jax.ShapeDtypeStruct((rows, rows), jnp.bfloat16),
            integers(1),
        ),
        [VMEM, VMEM],
        [],
        2,
        8,
        out_specs=(VMEM, VMEM, VMEM, SMEM),
    )(cell_nodes, kinetic)
    table, late_table = table.reshape(-1), late_table.reshape(-1)
    sent_short = jax.ShapeDtypeStruct((packed + packed // group_of(packed), LANES), jnp.int16)

    held_table = pltpu.SMEM((cells * stride,), jnp.int32)

    def shared(again, arrived, nodes, partial):
        return called(
            functools.partial(shared_kernel, sizes, slots, width, again),
            (sent_short, late_values),
            [SMEM, VMEM, SMEM, VMEM, VMEM, VMEM, VMEM],
            [spread, spread, spread, pairs_late, pairs_late, pairs_any, pairs_any]
            + [held_table, pltpu.SemaphoreType.DMA],
            6,
            11,
        )(regular, table, late_table, arrived, nodes, matrix, partial)

    def own(again, nodes):
        return called(
            functools.partial(own_kernel, sizes, again),
            (own_values, partial),
            [SMEM, VMEM, VMEM, VMEM],
            [held_table, pltpu.SemaphoreType.DMA((-(-cells // 8),))] + [pairs_own] * 8,
            10,
            4,
        )(regular, table, nodes, matrix)

    def scattered(again, values, late, arrived, nodes, *before):
        return called(
            functools.partial(scatter_kernel, sizes, slots, width, again),
            (wide,),
            [SMEM] + [VMEM] * (6 + len(before)),
            [pltpu.VMEM((2 * owned, LANES), jnp.float32)] + [pairs_own] * 4 + [spread, pairs_any, pairs_any]
            + [held_table, pltpu.SemaphoreType.DMA],
            18,
            14,
        )(regular, table, matrix, values, late, arrived, nodes, *before)[0]

    def begun_sums(again, send, nodes, *before):
        arrived = passed_along(send, "brick", -1)
        values, part = own(again, nodes)
        back, late_in = shared(again, arrived, nodes, part)
        returned = passed_along(back, "brick", 1)
        return scattered(again, values, late_in, arrived, nodes, *before), returned

    total, send = called(
        functools.partial(once_kernel, width),
        (wide, sent),
        [SMEM, VMEM, VMEM],
        [spread],
        3,
        6,
        input_output_aliases={1: 0},
    )(face_map, *begun_sums(False, send, begun))
    total, returned = begun_sums(True, send, total, begun)
    half = jax.ShapeDtypeStruct((width, owned // 2), jnp.bfloat16)
    total, first = called(
        functools.partial(twice_kernel, width),
        (wide, half),
        [SMEM, VMEM, VMEM],
        [spread],
        5,
        6,
        input_output_aliases={1: 0},
    )(face_map, total, returned)
    first_other = passed_along(first, "state", 1)
    (second,) = called(functools.partial(second_half_kernel, width), (half,), [VMEM], [], 2, 4)(total)
    second_other = passed_along(second, "state", 1)

    (gram,) = called(
        gram_own_kernel, (jax.ShapeDtypeStruct((width, width), jnp.float32),), [VMEM, VMEM], [], 1, 4
    )(first, second)
    (cross,) = called(
        cross_kernel, (jax.ShapeDtypeStruct((width // 2, width), jnp.float32),), [VMEM, VMEM], [], 1, 4
    )(first, first_other)
    slab = jax.ShapeDtypeStruct((width // 2, LANES), jnp.float32)
    slabs_held = pltpu.VMEM((4, width // 2, LANES), jnp.float32)
    pieces = called(functools.partial(gram_kernel, width), (slab,) * 4, [VMEM] * 4, [slabs_held], 1, 4)(
        gram, cross, second, second_other
    )
    mine = summed_over(pieces, "brick")
    theirs = [passed_along(piece, "state", 1) for piece in mine]
    (root,) = called(
        functools.partial(root_kernel, width),
        (jax.ShapeDtypeStruct((width, 2 * width), jnp.bfloat16),),
        [VMEM] * 8,
        [slabs_held, slabs_held],
        6,
        10,
    )(*mine, *theirs)
    pieces = 1
    return called(
        functools.partial(rotate_kernel, width, pieces),
        jax.ShapeDtypeStruct((width, owned), jnp.float32),
        [VMEM] * 5,
        [pltpu.VMEM((2, width, owned // 2 // pieces), jnp.float32), pltpu.SemaphoreType.DMA((2,))],
        3,
        8,
        out_specs=HBM,
    )(root, first, first_other, second, second_other)


def solution(mesh):
    in_specs = (P("state", "brick"), P(), P("brick"), P("brick", None), P("brick"))
    out_specs = P("state", "brick")
    return jax.shard_map(local, mesh=mesh, in_specs=in_specs, out_specs=out_specs, check_vma=False)
```
